32 devices in a mesh: tile: 8 (over z, x), kern: 4 (over y, core).
Axes of the slice: x: 2, y: 2, z: 4, core: 2. Of those that a mesh axis runs over, the one named last changes fastest.
Arguments:
- mask_logit: float32 [1024, 256], P('tile'), may hold values from -6 to 6
- target: int32 [1024, 256], P('tile'), may hold values 0 or 1
- kern_real: float32 [12, 65, 65], P('kern'), may hold values from -0.09375 to 0.09375
- kern_imag: float32 [12, 65, 65], P('kern'), may hold values from -0.09375 to 0.09375
- kern_weight: float32 [12], P('kern'), may hold values from 0.07 to 0.14
Outputs:
- logit_grad: float32 [1024, 256], P('tile', 'kern')
The draws below stay inside these ranges and needn't reach their ends.
All inputs are finite; a program needn't handle non-finite values. No bound on the sum of `target` on one device may be relied on, other than what follows from the above.
Results may differ from the reference program's by a relative error of at most 0.00021.
Values sent between devices are 32-bit elements; how exact they have to be, the bound alone decides.
No kernel may reach another device: no remote copies, remote signals or barrier semaphores. Data moves between devices by JAX's collectives and lax.ppermute only.
A program may use at most 64 MiB of HBM per device.

```python
import jax
import jax.numpy as jnp

COLS = 256
TAPS = 65
KERNELS = 12
ROWS = 1024


def place_ends(array, rng, smallest, high):
    dims = array.shape
    index_at = [jax.random.randint(jax.random.fold_in(rng, axis), (), 0, dims[axis]) for axis in range(len(dims))]
    array = array.at[tuple(index_at)].set(smallest)
    longest = dims.index(max(dims))
    index_at[longest] = (index_at[longest] + 1) % dims[longest]
    return array.at[tuple(index_at)].set(high)


def levels(rng, extent, cuts, least, top_value):
    level, own = 1.0, jax.random.fold_in(rng, 6)
    for dim, parts in cuts:
        steps = jnp.exp(jax.random.uniform(jax.random.fold_in(own, dim), (parts,), jnp.float32, least / len(cuts), top_value / len(cuts)))
        level = level * jnp.repeat(steps, extent[dim] // parts).reshape([-1 if axis == dim else 1 for axis in range(len(extent))])
    return level


def gaussian(key, dims, scale, reach, cuts=(), dtype=jnp.bfloat16):
    values = scale * jax.random.normal(key, dims, jnp.float32)
    if cuts:
        values = values * levels(key, dims, cuts, -0.22, 0.18)
    return jnp.clip(values, -reach, reach).astype(dtype)


def setup_inputs(seed: int = 0) -> dict:
    keys = jax.random.split(jax.random.key(seed), 6)
    return {
        "mask_logit": gaussian(keys[0], (ROWS, COLS), 1.0, 6.0, ((0, 8),), jnp.float32),
        "target": place_ends((jax.random.randint(keys[1], (ROWS, COLS), 0, 2) < 1).astype(jnp.int32), jax.random.fold_in(keys[1], 1), 0, 1),
        "kern_real": gaussian(keys[2], (KERNELS, TAPS, TAPS), (TAPS * TAPS) ** -0.5, 0.09375, ((0, 4),), jnp.float32),
        "kern_imag": gaussian(keys[3], (KERNELS, TAPS, TAPS), (TAPS * TAPS) ** -0.5, 0.09375, ((0, 4),), jnp.float32),
        "kern_weight": jnp.clip(0.07 + 0.07 * jax.random.uniform(keys[4], (KERNELS,), jnp.float32) ** levels(keys[4], (KERNELS,), ((0, 4),), -0.2, 0.2), 0.07, 0.14),
    }


MASK_SLOPE = 3.0
RESIST_SLOPE = 6.0
RESIST_LEVEL = 1.0

def place_taps(taps_grid, row_len, col_len, radius):
    tap_count = taps_grid.shape[0]
    flipped = taps_grid[::-1, ::-1]
    spread = jnp.pad(flipped, ((0, row_len - tap_count), (0, col_len - tap_count)))
    return jnp.roll(spread, (-radius, -radius), (0, 1))

def reference(mask_logit, target, kern_real, kern_imag, kern_weight):
    radius = (TAPS - 1) // 2
    row_total, col_total = mask_logit.shape
    target_value = target.astype(jnp.float32)

    def loss_of(logits):
        mask_value = jax.nn.sigmoid(MASK_SLOPE * logits)
        padded = jnp.pad(mask_value, radius)
        row_len, col_len = padded.shape
        spectrum = jnp.fft.fft2(padded)
        intensity = jnp.zeros_like(mask_value)
        for kernel_index in range(KERNELS):
            spread_real = place_taps(kern_real[kernel_index], row_len, col_len, radius)
            spread_imag = place_taps(kern_imag[kernel_index], row_len, col_len, radius)
            kernel_spec = jnp.fft.fft2(spread_real) + 1j * jnp.fft.fft2(spread_imag)
            light_field = jnp.fft.ifft2(spectrum * kernel_spec)[radius:radius + row_total, radius:radius + col_total]
            intensity = intensity + kern_weight[kernel_index] * (jnp.real(light_field) ** 2 + jnp.imag(light_field) ** 2)
        printed = jax.nn.sigmoid(RESIST_SLOPE * (intensity - RESIST_LEVEL))
        return jnp.sum((printed - target_value) ** 2)
    return jax.grad(loss_of)(mask_logit)
```

```python
import functools
import math

import jax
import jax.numpy as jnp
from jax import lax
from jax.experimental import pallas as pl
from jax.experimental.pallas import tpu as pltpu
from jax.sharding import PartitionSpec as P

MASK_SLOPE = 3.0
RESIST_SLOPE = 6.0
RESIST_LEVEL = 1.0

STEP = 64
SIZE = 128
TAP_ROWS = 72

F32 = jnp.float32
BF16 = jnp.bfloat16
TABLE_ROWS = (384, 512, 256, 512, 256, 256, 512, 256, 256)
BUFFERS = 3


def table_views(ref):
    views, at = [], 0
    for rows in TABLE_ROWS:
        views.append(ref.at[at:at + rows])
        at += rows
    return views


def split(value):
    high = value.astype(BF16)
    return high, (value - high.astype(F32)).astype(BF16)


def dot(left, right):
    return jnp.dot(left, right, preferred_element_type=F32)


def own_window(logit, place):
    cols = logit.shape[1]
    start = (place - 1) * STEP
    turned = pltpu.roll(jax.nn.sigmoid(MASK_SLOPE * logit), lax.rem(2 * cols - start, cols), 1)
    at = lax.broadcasted_iota(jnp.int32, logit.shape, 1) + start
    return jnp.where((at >= 0) & (at < cols), turned, 0.0)


def own_target(target, place):
    cols = target.shape[1]
    start = place * STEP - STEP // 2
    return pltpu.roll(target.astype(F32), lax.rem(2 * cols - start, cols), 1)[:, :SIZE]


def left_dot(table, value):
    rows = table.shape[0] // 2
    high, low = value
    both = dot(table[...], high)
    return both[:rows] + (both[rows:] + dot(table[0:rows], low))


def unit_waves():
    row = lax.broadcasted_iota(jnp.int32, (SIZE, SIZE), 0)
    col = lax.broadcasted_iota(jnp.int32, (SIZE, SIZE), 1)
    phase = (row * col) & (SIZE - 1)
    quarter = (phase + SIZE // 8) >> (SIZE.bit_length() - 3)
    rest = phase - quarter * (SIZE // 4)
    angle = rest.astype(F32) * (2.0 * math.pi / SIZE)
    square = angle * angle
    sin_near = cos_near = jnp.ones_like(angle)
    for step in (8, 6, 4, 2):
        sin_near = 1.0 - square * (1.0 / (step * (step + 1))) * sin_near
    for step in (10, 8, 6, 4, 2):
        cos_near = 1.0 - square * (1.0 / (step * (step - 1))) * cos_near
    sin_near = sin_near * angle
    turned = (quarter & 1) == 1
    cos_all = jnp.where(turned, -sin_near, cos_near)
    sin_all = jnp.where(turned, cos_near, sin_near)
    flip = (quarter & 2) == 2
    return jnp.where(flip, -cos_all, cos_all), jnp.where(flip, -sin_all, sin_all)


def table_kernel(table_ref):
    (
        taps_cols, taps_rows, mask_cols, rows_fwd, rows_inv, cols_inv, cols_fwd, grad_rows, grad_cols
    ) = table_views(table_ref)
    cos, sin = unit_waves()
    lane = lax.broadcasted_iota(jnp.int32, (SIZE, SIZE), 1)
    row = lax.broadcasted_iota(jnp.int32, (SIZE, SIZE), 0)
    left = lane < STEP
    scale = 1.0 / SIZE
    near, far = slice(0, STEP), slice(STEP, SIZE)

    def put(ref, blocks):
        rows = ref.shape[0] // 2
        at = 0
        for first, second in blocks:
            for column, value in enumerate((first, second)):
                for base, part in zip((0, rows), split(value)):
                    span = slice(column * SIZE, (column + 1) * SIZE)
                    ref[base + at:base + at + value.shape[0], span] = part
            at += first.shape[0]

    put(taps_cols.at[0:2 * SIZE], ((cos[near], sin[near]), (-sin[near], cos[near])))
    sign = (1 - 2 * (lane & 1)).astype(F32)
    even = (row & 1) == 0
    taps_cols[2 * SIZE:, :SIZE] = jnp.where(even, sign, 0.0).astype(BF16)
    taps_cols[2 * SIZE:, SIZE:] = jnp.where(even, 0.0, sign).astype(BF16)
    live = lane < SIZE - STEP + 1
    held = [[part.astype(F32) for part in split(jnp.where(live, wave, 0.0))] for wave in (cos, sin)]
    (cos_high, cos_low), (sin_high, sin_low) = held
    for phase, parts in enumerate((
        (cos_high, -sin_high, cos_high, -sin_high, cos_low, -sin_low),
        (sin_high, cos_high, sin_high, cos_high, sin_low, cos_low),
    )):
        for block in range(4):
            value = jnp.zeros((SIZE, SIZE), F32)
            for index, part in enumerate(parts):
                shift = index * TAP_ROWS - block * SIZE
                if -TAP_ROWS < shift < SIZE:
                    moved = pltpu.roll(part, shift % SIZE, 1) if shift % SIZE else part
                    value = jnp.where((lane >= shift) & (lane < shift + TAP_ROWS), moved, value)
            base = (block // 2) * 2 * SIZE + phase * SIZE
            span = slice((block % 2) * SIZE, (block % 2 + 1) * SIZE)
            taps_rows[base:base + SIZE, span] = value.astype(BF16)
    put(mask_cols, ((cos, -sin),))
    put(rows_fwd, ((cos, sin), (-sin, cos)))
    cos_s, sin_s = cos * scale, sin * scale
    put(rows_inv, ((cos_s[near], -sin_s[near]), (sin_s[near], cos_s[near])))
    cos_r, sin_r = pltpu.roll(cos_s, STEP, 1), pltpu.roll(sin_s, STEP, 1)
    for phase, value in enumerate((
        jnp.where(left, cos_s, sin_r), jnp.where(left, -sin_s, cos_r)
    )):
        for column, part in enumerate(split(value)):
            span = slice(column * SIZE, (column + 1) * SIZE)
            cols_inv[phase * SIZE:(phase + 1) * SIZE, span] = part
    put(cols_fwd, [
        pair for half in (near, far) for pair in ((cos[half], -sin[half]), (sin[half], cos[half]))
    ])
    put(grad_rows, ((cos_s[far], -sin_s[far]), (sin_s[far], cos_s[far])))
    for phase, (moved, value) in enumerate(((cos_r, cos_s), (-sin_r, -sin_s))):
        both = jnp.where(left, split(moved)[0].astype(F32), split(value)[1].astype(F32))
        grad_cols[phase * SIZE:(phase + 1) * SIZE, :SIZE] = both.astype(BF16)
        grad_cols[phase * SIZE:(phase + 1) * SIZE, SIZE:] = jnp.zeros((SIZE, SIZE), BF16)


def pack_kernel(weight_ref, logit_ref, target_ref, real_ref, imag_ref, even_ref, odd_ref, taps_ref):
    rows = logit_ref.shape[0]
    reach = SIZE - STEP
    half = reach // 2
    place = lax.axis_index("kern")
    to_next = lax.rem(lax.axis_index("tile"), 2) == 0
    window = own_window(logit_ref[...], place)
    wanted = own_target(target_ref[...], place)

    def packed(ref, near, near_target):
        ref[0:reach] = near[:, :SIZE]
        ref[reach:reach + half, :STEP] = near[:half, SIZE:SIZE + STEP]
        ref[reach:reach + half, STEP:] = near[half:, SIZE:SIZE + STEP]
        ref[reach + half:] = near_target

    top = window[0:reach]
    bottom = window[rows - reach:]
    top_target = wanted[0:half]
    bottom_target = wanted[rows - half:]
    packed(even_ref, jnp.where(to_next, bottom, top), jnp.where(to_next, bottom_target, top_target))
    packed(odd_ref, jnp.where(to_next, top, bottom), jnp.where(to_next, top_target, bottom_target))

    count = real_ref.shape[1]
    sublane = lax.broadcasted_iota(jnp.int32, (count, count), 0)
    lane = lax.broadcasted_iota(jnp.int32, (count, count), 1)
    taps_ref[...] = jnp.zeros_like(taps_ref)
    for kernel in range(real_ref.shape[0]):
        root = jnp.sqrt(jnp.full((1, count), weight_ref[kernel], F32))
        for part, ref in enumerate((real_ref, imag_ref)):
            taps = ref[kernel] * root
            taps_ref[kernel, 0:count, part * STEP:(part + 1) * STEP] = taps[:, :STEP]
            last = jnp.where(sublane == lane, taps[:, STEP:STEP + 1], 0.0)
            taps_ref[kernel, count + part:count + part + 1, 0:count] = jnp.sum(
                last, axis=0, keepdims=True
            )


def right_dot(value, table):
    high, low = split(value)
    rows = table.shape[0] // 2
    whole = jnp.concatenate([table[0:rows], table[0:rows], table[rows:]], axis=0)
    return dot(jnp.concatenate([high, low, high], axis=1), whole)


def tap_columns(blocks, work_t, taps_cols):
    tap_rows = blocks[0].shape[0]
    tap_count = SIZE - STEP + 1
    ends = [block[tap_count:tap_count + 2] for block in blocks]
    ends.append(jnp.zeros((STEP - 2 * len(blocks), SIZE), F32))
    ends = jnp.concatenate(ends, axis=0)
    turned = jnp.transpose(jnp.concatenate([ends, ends], axis=0))[:tap_rows]
    lane = lax.broadcasted_iota(jnp.int32, turned.shape, 1)
    coarse = turned.astype(BF16).astype(F32)
    turned = jnp.where(lane < STEP, coarse, turned - coarse)
    owner = (lane & (STEP - 1)) >> 1
    for index, block in enumerate(blocks):
        part = slice(index * tap_rows, (index + 1) * tap_rows)
        high, low = split(block)
        work_t[part, 0:128] = high
        work_t[part, 128:256] = low
        work_t[part, 256:384] = high
        work_t[part, 384:512] = jnp.where(owner == index, turned, 0.0).astype(BF16)
    table = [taps_cols[at * SIZE:(at + 1) * SIZE] for at in (0, 0, 1, 2)]
    return dot(work_t[0:len(blocks) * tap_rows], jnp.concatenate(table, axis=0))


def tap_spectra(mixed, indices, taps_rows, store):
    columns = []
    for index in indices:
        part = slice(index * TAP_ROWS, (index + 1) * TAP_ROWS)
        columns.append(jnp.concatenate([mixed[part, :SIZE], mixed[part, SIZE:]], axis=0))
    high, low = split(jnp.concatenate(columns, axis=1))
    wide = jnp.concatenate([taps_rows[0:2 * SIZE], taps_rows[2 * SIZE:]], axis=1)
    spectra = dot(wide[:, :6 * TAP_ROWS], jnp.concatenate([high, low, high], axis=0))
    for place, index in enumerate(indices):
        store(index, spectra[:, place * SIZE:(place + 1) * SIZE])


def field_products(spectrum, mask_spec, work, slot):
    for side in range(2):
        cut = slice(side * SIZE, (side + 1) * SIZE)
        to = slice((2 * slot + side) * SIZE, (2 * slot + side + 1) * SIZE)
        kern_re = spectrum[0:SIZE]
        kern_im = spectrum[SIZE:]
        mask_re = mask_spec[0:SIZE, cut]
        mask_im = mask_spec[SIZE:, cut]
        high, low = split(mask_re * kern_re - mask_im * kern_im)
        work[0, 0:SIZE, to] = high
        work[1, 0:SIZE, to] = low
        high, low = split(mask_re * kern_im + mask_im * kern_re)
        work[0, SIZE:, to] = high
        work[1, SIZE:, to] = low


def field_rows_step(work, work_z, windows, rows_inv):
    width = windows * 2 * SIZE
    high, low = split(left_dot(rows_inv, (work[0, :, 0:width], work[1, :, 0:width])))
    for piece in range(windows * 2):
        cut = slice(piece * SIZE, (piece + 1) * SIZE)
        at = slice(piece * STEP, (piece + 1) * STEP)
        work_z[0, at, 0:SIZE] = high[0:STEP, cut]
        work_z[0, at, SIZE:] = high[STEP:, cut]
        work_z[1, at, 0:SIZE] = low[0:STEP, cut]
        work_z[1, at, SIZE:] = low[STEP:, cut]


def field_cols_step(work_z, windows, cols_inv):
    pieces = windows * 2
    major = dot(work_z[0, 0:pieces * STEP], cols_inv[...])
    minor = dot(work_z[1, 0:pieces * STEP], cols_inv[:, 0:SIZE])
    result = major[:, 0:SIZE] + (major[:, SIZE:] + minor)
    return [
        [result[(index * 2 + side) * STEP:(index * 2 + side + 1) * STEP] for side in range(2)]
        for index in range(windows)
    ]


def all_spectra(blocks, work_t, taps_cols, taps_rows, out):
    mixed = tap_columns(blocks, work_t, taps_cols)

    def store(index, value):
        out[index] = value

    for first in range(0, len(blocks), 2):
        tap_spectra(mixed, range(first, min(first + 2, len(blocks))), taps_rows, store)


def all_fields(todo, spectra, mask_specs, work_x, work_z, rows_inv, cols_inv, take):
    def products(at):
        kernel, windows = todo[at]
        for slot, window in enumerate(windows):
            field_products(spectra[kernel], mask_specs[window], work_x.at[at % BUFFERS], slot)

    products(0)
    for at in range(len(todo) + 1):
        if at + 1 < len(todo):
            products(at + 1)
        if at < len(todo):
            buffer = at % BUFFERS
            field_rows_step(work_x.at[buffer], work_z.at[buffer], len(todo[at][1]), rows_inv)
        if at > 0:
            kernel, windows = todo[at - 1]
            pieces = field_cols_step(work_z.at[(at - 1) % BUFFERS], len(windows), cols_inv)
            for index, pair in zip(windows, pieces):
                take(kernel, index, pair)


def local_kernel(
    logit_ref, taps0, taps1, taps2, table_ref,
    spectra, own_cols, mid_spec, mid_fields, mid_total,
    work_t, work_x, work_z,
):
    taps_cols, taps_rows, mask_cols, rows_fwd, rows_inv, cols_inv = table_views(table_ref)[:6]
    rows, cols = logit_ref.shape
    own = own_window(logit_ref[...], lax.axis_index("kern"))
    for side in range(2):
        window = own[:, :SIZE] if side == 0 else pltpu.roll(own, cols - STEP, 1)[:, :SIZE]
        mixed = right_dot(window, mask_cols)
        span = slice(side * SIZE, (side + 1) * SIZE)
        for half_at, part in enumerate(split(mixed)):
            own_cols[half_at, 0, :, span] = part[:, :SIZE]
            own_cols[half_at, 1, :, span] = part[:, SIZE:]
    mid_spec[...] = left_dot(
        rows_fwd,
        (own_cols[0].reshape(2 * rows, 2 * SIZE), own_cols[1].reshape(2 * rows, 2 * SIZE)),
    )
    blocks = [ref[kernel] for ref in (taps0, taps1, taps2) for kernel in range(ref.shape[0])]
    all_spectra(blocks, work_t, taps_cols, taps_rows, spectra)
    mid_total[...] = jnp.zeros_like(mid_total)

    def take(kernel, index, pair):
        for side, piece in enumerate(pair):
            cut = slice(side * SIZE, (side + 1) * SIZE)
            mid_fields[kernel, :, cut] = piece
            mid_total[:, cut] += piece * piece

    all_fields(
        [(kernel, (1,)) for kernel in range(len(blocks))],
        [spectra.at[kernel] for kernel in range(len(blocks))],
        {1: mid_spec}, work_x, work_z, rows_inv, cols_inv, take,
    )


def main_kernel(
    logit_ref, target_ref, even_ref, odd_ref, taps3, table_ref,
    early_spectra, own_cols, mid_spec, mid_fields, mid_total,
    out_ref,
    late_spectra, mask_spec, fields, total, slope, work_t, work_x, work_z, work_b, grad_spec,
):
    (
        taps_cols, taps_rows, mask_cols, rows_fwd, rows_inv, cols_inv, cols_fwd, grad_rows, grad_cols
    ) = table_views(table_ref)
    rows, cols = logit_ref.shape
    reach = SIZE - STEP
    half = reach // 2
    place = lax.axis_index("kern")
    band = lax.axis_index("tile")
    bands = lax.axis_size("tile")
    field_rows = rows + reach
    windows = field_rows // STEP
    outs = rows // STEP
    early = early_spectra.shape[0]
    late = taps3.shape[0]
    count = early + late
    pairs = count // 2
    spectra = [early_spectra.at[kernel] for kernel in range(early)]
    spectra += [late_spectra.at[kernel] for kernel in range(late)]

    even = lax.rem(band, 2) == 0
    above = jnp.where(even, odd_ref[...], even_ref[...])
    below = jnp.where(even, even_ref[...], odd_ref[...])
    lane = lax.broadcasted_iota(jnp.int32, (half, SIZE), 1)

    def second(block):
        outer = block[reach:reach + half]
        inner = pltpu.roll(block[0:reach], STEP, 1)
        return jnp.concatenate(
            [
                jnp.where(lane < STEP, inner[:half], pltpu.roll(outer, STEP, 1)),
                jnp.where(lane < STEP, inner[half:], outer),
            ],
            axis=0,
        )

    sides = (
        jnp.concatenate([above[0:reach], below[0:reach]], axis=0),
        jnp.concatenate([second(above), second(below)], axis=0),
    )
    for side, window in enumerate(sides):
        mixed = right_dot(window, mask_cols)
        for half_at, part in enumerate(split(mixed)):
            for phase in range(2):
                cut = slice(phase * SIZE, (phase + 1) * SIZE)
                base = phase * SIZE
                span = slice(side * SIZE, (side + 1) * SIZE)
                work_x[0, half_at, base:base + reach, span] = part[:reach, cut]
                span = slice((2 + side) * SIZE, (3 + side) * SIZE)
                work_x[0, half_at, base + STEP:base + SIZE, span] = part[reach:, cut]
    for half_at in range(2):
        for phase in range(2):
            base = phase * SIZE
            span = slice(0, 2 * SIZE)
            work_x[0, half_at, base + reach:base + SIZE, span] = own_cols[half_at, phase, 0:STEP]
            span = slice(2 * SIZE, 4 * SIZE)
            work_x[0, half_at, base:base + STEP, span] = own_cols[half_at, phase, rows - STEP:]
    outer = left_dot(rows_fwd, (work_x[0, 0, :, 0:4 * SIZE], work_x[0, 1, :, 0:4 * SIZE]))
    mask_spec[0] = outer[:, 0:2 * SIZE]
    mask_spec[1] = outer[:, 2 * SIZE:]

    all_spectra([taps3[kernel] for kernel in range(late)], work_t, taps_cols, taps_rows, late_spectra)

    total[0:STEP] = jnp.zeros((STEP, 2 * SIZE), F32)
    total[STEP:2 * STEP] = mid_total[...]
    total[2 * STEP:] = jnp.zeros((STEP, 2 * SIZE), F32)

    def take(kernel, index, pair):
        at_rows = slice(index * STEP, (index + 1) * STEP)
        for side, piece in enumerate(pair):
            cut = slice(side * SIZE, (side + 1) * SIZE)
            fields[kernel, at_rows, cut] = piece
            total[at_rows, cut] += piece * piece

    all_fields(
        [(kernel, (0, 2) if kernel < early else (0, 1, 2)) for kernel in range(count)],
        spectra, {0: mask_spec.at[0], 1: mid_spec, 2: mask_spec.at[1]},
        work_x, work_z, rows_inv, cols_inv, take,
    )

    def field(kernel):
        if kernel >= early:
            return fields[kernel]
        return jnp.concatenate(
            [fields[kernel, 0:STEP], mid_fields[kernel], fields[kernel, 2 * STEP:]], axis=0
        )

    target_near = jnp.concatenate(
        [above[reach + half:], own_target(target_ref[...], place), below[reach + half:]], axis=0
    )
    start = place * STEP - half
    target_turned = pltpu.roll(target_near, STEP, 1)
    lane = lax.broadcasted_iota(jnp.int32, (field_rows, SIZE), 1)
    row = lax.broadcasted_iota(jnp.int32, (field_rows, SIZE), 0) + band * rows - half
    first = lane < STEP
    low_lane = lane & (STEP - 1)
    for side in range(2):
        cut = slice(side * SIZE, (side + 1) * SIZE)
        squares = total[:, cut]
        intensity = squares + pltpu.roll(squares, STEP, 1)
        if side == 0:
            wanted = jnp.where(first, target_near, target_turned)
        else:
            wanted = jnp.where(first, target_turned, target_near)
        printed = jax.nn.sigmoid(RESIST_SLOPE * (intensity - RESIST_LEVEL))
        at = low_lane + (start + side * STEP)
        valid = (at >= 0) & (at < cols) & (row >= 0) & (row < bands * rows)
        slope[:, cut] = jnp.where(
            valid, (2.0 * RESIST_SLOPE) * (printed - wanted) * printed * (1.0 - printed), 0.0
        )

    grad_spec[...] = jnp.zeros_like(grad_spec)

    def grad_cols_step(pair):
        buffer = pair % BUFFERS
        value = jnp.concatenate(
            [slope[...] * field(2 * pair + member) for member in range(2)], axis=0
        )
        high, low = split(value)
        mixed = dot(high, cols_fwd[0:256]) + (
            dot(high, cols_fwd[256:]) + dot(low, cols_fwd[0:256])
        )
        for half_at, part in enumerate(split(mixed)):
            for index in range(outs):
                for member in range(2):
                    base = member * field_rows + index * STEP
                    at = slice(base, base + SIZE)
                    base = (2 * index + member) * SIZE
                    span = slice(base, base + SIZE)
                    work_b[buffer, half_at, 0:SIZE, span] = part[at, :SIZE]
                    work_b[buffer, half_at, SIZE:, span] = part[at, SIZE:]

    def grad_rows_step(pair):
        buffer = pair % BUFFERS
        spec = left_dot(rows_fwd, (work_b[buffer, 0], work_b[buffer, 1]))
        for index in range(outs):
            cut = slice(index * SIZE, (index + 1) * SIZE)
            sum_re = grad_spec[0:SIZE, cut]
            sum_im = grad_spec[SIZE:, cut]
            for member in range(2):
                base = (2 * index + member) * SIZE
                span = slice(base, base + SIZE)
                kern_re = spectra[2 * pair + member][0:SIZE]
                kern_im = spectra[2 * pair + member][SIZE:]
                spec_re = spec[0:SIZE, span]
                spec_im = spec[SIZE:, span]
                sum_re = sum_re + kern_re * spec_re + kern_im * spec_im
                sum_im = sum_im + kern_re * spec_im - kern_im * spec_re
            grad_spec[0:SIZE, cut] = sum_re
            grad_spec[SIZE:, cut] = sum_im

    for pair in range(pairs + 1):
        if pair < pairs:
            grad_cols_step(pair)
        if pair > 0:
            grad_rows_step(pair - 1)

    halfway = left_dot(grad_rows, split(grad_spec[...]))
    stacked = jnp.concatenate(
        [
            jnp.concatenate(
                [
                    halfway[0:STEP, index * SIZE:(index + 1) * SIZE],
                    halfway[STEP:, index * SIZE:(index + 1) * SIZE],
                ],
                axis=1,
            )
            for index in range(outs)
        ],
        axis=0,
    )
    high, low = split(stacked)
    both = dot(high, grad_cols[:, :SIZE])
    gradient = both[:, :STEP] + (both[:, STEP:] + dot(low, grad_cols[:, :STEP]))
    mask_share = pltpu.roll(
        jax.nn.sigmoid(MASK_SLOPE * logit_ref[...]), lax.rem(cols - place * STEP, cols), 1
    )[:, :STEP]
    out_ref[...] = jnp.transpose(
        gradient * (2.0 * MASK_SLOPE) * mask_share * (1.0 - mask_share)
    )


def body(mask_logit, target, kern_real, kern_imag, kern_weight):
    rows, cols = mask_logit.shape
    local, tap_count, _ = kern_real.shape
    reach = tap_count - 1
    kern_size = lax.axis_size("kern")
    tile_size = lax.axis_size("tile")
    assert reach == SIZE - STEP and cols == STEP * kern_size and rows % STEP == 0
    assert kern_size == 4 and rows == SIZE
    half = reach // 2
    vmem = pl.BlockSpec(memory_space=pltpu.VMEM)
    smem = pl.BlockSpec(memory_space=pltpu.SMEM)


    even, odd, taps = pl.pallas_call(
        pack_kernel,
        out_shape=(
            jax.ShapeDtypeStruct((2 * reach, SIZE), F32),
            jax.ShapeDtypeStruct((2 * reach, SIZE), F32),
            jax.ShapeDtypeStruct((local, TAP_ROWS, SIZE), F32),
        ),
        in_specs=[smem] + [vmem] * 4,
        out_specs=(vmem,) * 3,
    )(kern_weight, mask_logit, target, kern_real, kern_imag)

    def swaps(first):
        return [p for i in range(first, tile_size - 1, 2) for p in ((i, i + 1), (i + 1, i))]

    def flipped(value, flip):
        return lax.ppermute(value, "kern", [(i, i ^ flip) for i in range(kern_size)])

    far = flipped(taps, 2)
    near = flipped(taps, 1)
    even = lax.ppermute(even, "tile", swaps(0))
    odd = lax.ppermute(odd, "tile", swaps(1))
    both = flipped(far, 1)

    table = pl.pallas_call(
        table_kernel,
        out_shape=jax.ShapeDtypeStruct((sum(TABLE_ROWS), 2 * SIZE), BF16),
        out_specs=vmem,
        compiler_params=pltpu.CompilerParams(vmem_limit_bytes=8 * 1024 * 1024),
        cost_estimate=pl.CostEstimate(flops=2 * 10**9, bytes_accessed=5 * 10**6, transcendentals=0),
    )()
    field_rows = rows + reach
    windows = field_rows // STEP
    outs = rows // STEP
    count = local * kern_size
    early = count - local
    local_out = pl.pallas_call(
        local_kernel,
        out_shape=(
            jax.ShapeDtypeStruct((early, 2 * SIZE, SIZE), F32),
            jax.ShapeDtypeStruct((2, 2, rows, 2 * SIZE), BF16),
            jax.ShapeDtypeStruct((2 * SIZE, 2 * SIZE), F32),
            jax.ShapeDtypeStruct((early, STEP, 2 * SIZE), F32),
            jax.ShapeDtypeStruct((STEP, 2 * SIZE), F32),
        ),
        in_specs=[vmem] * 5,
        out_specs=(vmem,) * 5,
        scratch_shapes=[
            pltpu.VMEM((early * TAP_ROWS, 4 * SIZE), BF16),
            pltpu.VMEM((BUFFERS, 2, 2 * SIZE, 2 * SIZE), BF16),
            pltpu.VMEM((BUFFERS, 2, 2 * STEP, 2 * SIZE), BF16),
        ],
        compiler_params=pltpu.CompilerParams(vmem_limit_bytes=16 * 1024 * 1024),
        cost_estimate=pl.CostEstimate(flops=4 * 10**9, bytes_accessed=5 * 10**6, transcendentals=0),
    )(mask_logit, taps, near, far, table)
    result = pl.pallas_call(
        main_kernel,
        out_shape=jax.ShapeDtypeStruct((STEP, rows), F32),
        in_specs=[vmem] * (6 + len(local_out)),
        out_specs=vmem,
        scratch_shapes=[
            pltpu.VMEM((local, 2 * SIZE, SIZE), F32),
            pltpu.VMEM((2, 2 * SIZE, 2 * SIZE), F32),
            pltpu.VMEM((count, field_rows, 2 * SIZE), F32),
            pltpu.VMEM((field_rows, 2 * SIZE), F32),
            pltpu.VMEM((field_rows, 2 * SIZE), F32),
            pltpu.VMEM((local * TAP_ROWS, 4 * SIZE), BF16),
            pltpu.VMEM((BUFFERS, 2, 2 * SIZE, 2 * windows * SIZE), BF16),
            pltpu.VMEM((BUFFERS, 2, 2 * windows * STEP, 2 * SIZE), BF16),
            pltpu.VMEM((BUFFERS, 2, 2 * SIZE, 2 * outs * SIZE), BF16),
            pltpu.VMEM((2 * SIZE, outs * SIZE), F32),
        ],
        compiler_params=pltpu.CompilerParams(vmem_limit_bytes=24 * 1024 * 1024),
    )(mask_logit, target, even, odd, both, table, *local_out)
    return jnp.transpose(result)


def solution(mesh):
    in_specs = (
        P("tile", None),
        P("tile", None),
        P("kern", None, None),
        P("kern", None, None),
        P("kern"),
    )
    out_specs = P("tile", "kern")
    return jax.shard_map(body, mesh=mesh, in_specs=in_specs, out_specs=out_specs, check_vma=False)
```

```python
import functools
import math

import jax
import jax.numpy as jnp
from jax import lax
from jax.experimental import pallas as pl
from jax.experimental.pallas import tpu as pltpu
from jax.sharding import PartitionSpec as P

MASK_SLOPE = 3.0
RESIST_SLOPE = 6.0
RESIST_LEVEL = 1.0

STEP = 64
SIZE = 128
TAP_ROWS = 72

F32 = jnp.float32
BF16 = jnp.bfloat16
TABLE_ROWS = (384, 512, 256, 512, 256, 256, 512, 256, 256)
BUFFERS = 3


def table_views(ref):
    views, at = [], 0
    for rows in TABLE_ROWS:
        views.append(ref.at[at:at + rows])
        at += rows
    return views


def split(value):
    high = value.astype(BF16)
    return high, (value - high.astype(F32)).astype(BF16)


def dot(left, right):
    return jnp.dot(left, right, preferred_element_type=F32)


def own_window(logit, place):
    cols = logit.shape[1]
    start = (place - 1) * STEP
    turned = pltpu.roll(jax.nn.sigmoid(MASK_SLOPE * logit), lax.rem(2 * cols - start, cols), 1)
    at = lax.broadcasted_iota(jnp.int32, logit.shape, 1) + start
    return jnp.where((at >= 0) & (at < cols), turned, 0.0)


def own_target(target, place):
    cols = target.shape[1]
    start = place * STEP - STEP // 2
    return pltpu.roll(target.astype(F32), lax.rem(2 * cols - start, cols), 1)[:, :SIZE]


def left_dot(table, value):
    rows = table.shape[0] // 2
    high, low = value
    both = dot(table[...], high)
    return both[:rows] + (both[rows:] + dot(table[0:rows], low))


def unit_waves():
    row = lax.broadcasted_iota(jnp.int32, (SIZE, SIZE), 0)
    col = lax.broadcasted_iota(jnp.int32, (SIZE, SIZE), 1)
    phase = (row * col) & (SIZE - 1)
    quarter = (phase + SIZE // 8) >> (SIZE.bit_length() - 3)
    rest = phase - quarter * (SIZE // 4)
    angle = rest.astype(F32) * (2.0 * math.pi / SIZE)
    square = angle * angle
    sin_near = cos_near = jnp.ones_like(angle)
    for step in (8, 6, 4, 2):
        sin_near = 1.0 - square * (1.0 / (step * (step + 1))) * sin_near
    for step in (10, 8, 6, 4, 2):
        cos_near = 1.0 - square * (1.0 / (step * (step - 1))) * cos_near
    sin_near = sin_near * angle
    turned = (quarter & 1) == 1
    cos_all = jnp.where(turned, -sin_near, cos_near)
    sin_all = jnp.where(turned, cos_near, sin_near)
    flip = (quarter & 2) == 2
    return jnp.where(flip, -cos_all, cos_all), jnp.where(flip, -sin_all, sin_all)


def table_kernel(table_ref):
    (
        taps_cols, taps_rows, mask_cols, rows_fwd, rows_inv, cols_inv, cols_fwd, grad_rows, grad_cols
    ) = table_views(table_ref)
    cos, sin = unit_waves()
    lane = lax.broadcasted_iota(jnp.int32, (SIZE, SIZE), 1)
    row = lax.broadcasted_iota(jnp.int32, (SIZE, SIZE), 0)
    left = lane < STEP
    scale = 1.0 / SIZE
    near, far = slice(0, STEP), slice(STEP, SIZE)

    def put(ref, blocks):
        rows = ref.shape[0] // 2
        at = 0
        for first, second in blocks:
            for column, value in enumerate((first, second)):
                for base, part in zip((0, rows), split(value)):
                    span = slice(column * SIZE, (column + 1) * SIZE)
                    ref[base + at:base + at + value.shape[0], span] = part
            at += first.shape[0]

    put(taps_cols.at[0:2 * SIZE], ((cos[near], sin[near]), (-sin[near], cos[near])))
    sign = (1 - 2 * (lane & 1)).astype(F32)
    even = (row & 1) == 0
    taps_cols[2 * SIZE:, :SIZE] = jnp.where(even, sign, 0.0).astype(BF16)
    taps_cols[2 * SIZE:, SIZE:] = jnp.where(even, 0.0, sign).astype(BF16)
    live = lane < SIZE - STEP + 1
    held = [[part.astype(F32) for part in split(jnp.where(live, wave, 0.0))] for wave in (cos, sin)]
    (cos_high, cos_low), (sin_high, sin_low) = held
    for phase, parts in enumerate((
        (cos_high, -sin_high, cos_high, -sin_high, cos_low, -sin_low),
        (sin_high, cos_high, sin_high, cos_high, sin_low, cos_low),
    )):
        for block in range(4):
            value = jnp.zeros((SIZE, SIZE), F32)
            for index, part in enumerate(parts):
                shift = index * TAP_ROWS - block * SIZE
                if -TAP_ROWS < shift < SIZE:
                    moved = pltpu.roll(part, shift % SIZE, 1) if shift % SIZE else part
                    value = jnp.where((lane >= shift) & (lane < shift + TAP_ROWS), moved, value)
            base = (block // 2) * 2 * SIZE + phase * SIZE
            span = slice((block % 2) * SIZE, (block % 2 + 1) * SIZE)
            taps_rows[base:base + SIZE, span] = value.astype(BF16)
    put(mask_cols, ((cos, -sin),))
    put(rows_fwd, ((cos, sin), (-sin, cos)))
    cos_s, sin_s = cos * scale, sin * scale
    put(rows_inv, ((cos_s[near], -sin_s[near]), (sin_s[near], cos_s[near])))
    cos_r, sin_r = pltpu.roll(cos_s, STEP, 1), pltpu.roll(sin_s, STEP, 1)
    for phase, value in enumerate((
        jnp.where(left, cos_s, sin_r), jnp.where(left, -sin_s, cos_r)
    )):
        for column, part in enumerate(split(value)):
            span = slice(column * SIZE, (column + 1) * SIZE)
            cols_inv[phase * SIZE:(phase + 1) * SIZE, span] = part
    put(cols_fwd, [
        pair for half in (near, far) for pair in ((cos[half], -sin[half]), (sin[half], cos[half]))
    ])
    put(grad_rows, ((cos_s[far], -sin_s[far]), (sin_s[far], cos_s[far])))
    for phase, (moved, value) in enumerate(((cos_r, cos_s), (-sin_r, -sin_s))):
        both = jnp.where(left, split(moved)[0].astype(F32), split(value)[1].astype(F32))
        grad_cols[phase * SIZE:(phase + 1) * SIZE, :SIZE] = both.astype(BF16)
        grad_cols[phase * SIZE:(phase + 1) * SIZE, SIZE:] = jnp.zeros((SIZE, SIZE), BF16)


def pack_kernel(weight_ref, logit_ref, target_ref, real_ref, imag_ref, even_ref, odd_ref, taps_ref):
    rows = logit_ref.shape[0]
    reach = SIZE - STEP
    half = reach // 2
    place = lax.axis_index("kern")
    to_next = lax.rem(lax.axis_index("tile"), 2) == 0
    window = own_window(logit_ref[...], place)
    wanted = own_target(target_ref[...], place)

    def packed(ref, near, near_target):
        ref[0:reach] = near[:, :SIZE]
        ref[reach:reach + half, :STEP] = near[:half, SIZE:SIZE + STEP]
        ref[reach:reach + half, STEP:] = near[half:, SIZE:SIZE + STEP]
        ref[reach + half:] = near_target

    top = window[0:reach]
    bottom = window[rows - reach:]
    top_target = wanted[0:half]
    bottom_target = wanted[rows - half:]
    packed(even_ref, jnp.where(to_next, bottom, top), jnp.where(to_next, bottom_target, top_target))
    packed(odd_ref, jnp.where(to_next, top, bottom), jnp.where(to_next, top_target, bottom_target))

    count = real_ref.shape[1]
    sublane = lax.broadcasted_iota(jnp.int32, (count, count), 0)
    lane = lax.broadcasted_iota(jnp.int32, (count, count), 1)
    taps_ref[...] = jnp.zeros_like(taps_ref)
    for kernel in range(real_ref.shape[0]):
        root = jnp.sqrt(jnp.full((1, count), weight_ref[kernel], F32))
        for part, ref in enumerate((real_ref, imag_ref)):
            taps = ref[kernel] * root
            taps_ref[kernel, 0:count, part * STEP:(part + 1) * STEP] = taps[:, :STEP]
            last = jnp.where(sublane == lane, taps[:, STEP:STEP + 1], 0.0)
            taps_ref[kernel, count + part:count + part + 1, 0:count] = jnp.sum(
                last, axis=0, keepdims=True
            )


def right_dot(value, table):
    high, low = split(value)
    rows = table.shape[0] // 2
    whole = jnp.concatenate([table[0:rows], table[0:rows], table[rows:]], axis=0)
    return dot(jnp.concatenate([high, low, high], axis=1), whole)


def tap_columns(blocks, work_t, taps_cols):
    tap_rows = blocks[0].shape[0]
    tap_count = SIZE - STEP + 1
    ends = [block[tap_count:tap_count + 2] for block in blocks]
    ends.append(jnp.zeros((STEP - 2 * len(blocks), SIZE), F32))
    ends = jnp.concatenate(ends, axis=0)
    turned = jnp.transpose(jnp.concatenate([ends, ends], axis=0))[:tap_rows]
    lane = lax.broadcasted_iota(jnp.int32, turned.shape, 1)
    coarse = turned.astype(BF16).astype(F32)
    turned = jnp.where(lane < STEP, coarse, turned - coarse)
    owner = (lane & (STEP - 1)) >> 1
    for index, block in enumerate(blocks):
        part = slice(index * tap_rows, (index + 1) * tap_rows)
        high, low = split(block)
        work_t[part, 0:128] = high
        work_t[part, 128:256] = low
        work_t[part, 256:384] = high
        work_t[part, 384:512] = jnp.where(owner == index, turned, 0.0).astype(BF16)
    table = [taps_cols[at * SIZE:(at + 1) * SIZE] for at in (0, 0, 1, 2)]
    return dot(work_t[0:len(blocks) * tap_rows], jnp.concatenate(table, axis=0))


def tap_spectra(mixed, indices, taps_rows, store):
    columns = []
    for index in indices:
        part = slice(index * TAP_ROWS, (index + 1) * TAP_ROWS)
        columns.append(jnp.concatenate([mixed[part, :SIZE], mixed[part, SIZE:]], axis=0))
    high, low = split(jnp.concatenate(columns, axis=1))
    wide = jnp.concatenate([taps_rows[0:2 * SIZE], taps_rows[2 * SIZE:]], axis=1)
    spectra = dot(wide[:, :6 * TAP_ROWS], jnp.concatenate([high, low, high], axis=0))
    for place, index in enumerate(indices):
        store(index, spectra[:, place * SIZE:(place + 1) * SIZE])


def field_products(spectrum, mask_spec, work):
    for side in range(2):
        cut = slice(side * SIZE, (side + 1) * SIZE)
        kern_re = spectrum[0:SIZE]
        kern_im = spectrum[SIZE:]
        mask_re = mask_spec[0:SIZE, cut]
        mask_im = mask_spec[SIZE:, cut]
        high, low = split(mask_re * kern_re - mask_im * kern_im)
        work[0, 0:SIZE, cut] = high
        work[1, 0:SIZE, cut] = low
        high, low = split(mask_re * kern_im + mask_im * kern_re)
        work[0, SIZE:, cut] = high
        work[1, SIZE:, cut] = low


def field_rows_step(work, work_z, index, rows_inv):
    high, low = split(left_dot(rows_inv, (work[0], work[1])))
    for side in range(2):
        cut = slice(side * SIZE, (side + 1) * SIZE)
        base = (index * 2 + side) * STEP
        at = slice(base, base + STEP)
        work_z[0, at, 0:SIZE] = high[0:STEP, cut]
        work_z[0, at, SIZE:] = high[STEP:, cut]
        work_z[1, at, 0:SIZE] = low[0:STEP, cut]
        work_z[1, at, SIZE:] = low[STEP:, cut]


def field_cols_step(work_z, windows, cols_inv):
    pieces = windows * 2
    major = dot(work_z[0, 0:pieces * STEP], cols_inv[...])
    minor = dot(work_z[1, 0:pieces * STEP], cols_inv[:, 0:SIZE])
    result = major[:, 0:SIZE] + (major[:, SIZE:] + minor)
    return [
        [result[(index * 2 + side) * STEP:(index * 2 + side + 1) * STEP] for side in range(2)]
        for index in range(windows)
    ]


def all_spectra(blocks, work_t, taps_cols, taps_rows, out):
    mixed = tap_columns(blocks, work_t, taps_cols)

    def store(index, value):
        out[index] = value

    for first in range(0, len(blocks), 2):
        tap_spectra(mixed, range(first, min(first + 2, len(blocks))), taps_rows, store)


def all_fields(todo, spectra, mask_specs, work_x, work_z, rows_inv, cols_inv, take):
    def products(at, slot):
        kernel, windows = todo[at]
        field_products(
            spectra[kernel], mask_specs[windows[slot]], work_x.at[at % BUFFERS, slot]
        )

    for slot in range(len(todo[0][1])):
        products(0, slot)
    for at in range(len(todo) + 1):
        later = len(todo[at + 1][1]) if at + 1 < len(todo) else 0
        now = len(todo[at][1]) if at < len(todo) else 0
        for slot in range(max(later, now)):
            if slot < later:
                products(at + 1, slot)
            if slot < now:
                buffer = at % BUFFERS
                field_rows_step(work_x.at[buffer, slot], work_z.at[buffer], slot, rows_inv)
        if at > 0:
            kernel, windows = todo[at - 1]
            pieces = field_cols_step(work_z.at[(at - 1) % BUFFERS], len(windows), cols_inv)
            for index, pair in zip(windows, pieces):
                take(kernel, index, pair)


def local_kernel(
    logit_ref, taps0, taps1, taps2, table_ref,
    spectra, own_cols, mid_spec, mid_fields, mid_total,
    work_t, work_x, work_z,
):
    taps_cols, taps_rows, mask_cols, rows_fwd, rows_inv, cols_inv = table_views(table_ref)[:6]
    rows, cols = logit_ref.shape
    own = own_window(logit_ref[...], lax.axis_index("kern"))
    for side in range(2):
        window = own[:, :SIZE] if side == 0 else pltpu.roll(own, cols - STEP, 1)[:, :SIZE]
        mixed = right_dot(window, mask_cols)
        span = slice(side * SIZE, (side + 1) * SIZE)
        for half_at, part in enumerate(split(mixed)):
            own_cols[half_at, 0, :, span] = part[:, :SIZE]
            own_cols[half_at, 1, :, span] = part[:, SIZE:]
    mid_spec[...] = left_dot(
        rows_fwd,
        (own_cols[0].reshape(2 * rows, 2 * SIZE), own_cols[1].reshape(2 * rows, 2 * SIZE)),
    )
    blocks = [ref[kernel] for ref in (taps0, taps1, taps2) for kernel in range(ref.shape[0])]
    all_spectra(blocks, work_t, taps_cols, taps_rows, spectra)
    mid_total[...] = jnp.zeros_like(mid_total)

    def take(kernel, index, pair):
        for side, piece in enumerate(pair):
            cut = slice(side * SIZE, (side + 1) * SIZE)
            mid_fields[kernel, :, cut] = piece
            mid_total[:, cut] += piece * piece

    all_fields(
        [(kernel, (1,)) for kernel in range(len(blocks))],
        [spectra.at[kernel] for kernel in range(len(blocks))],
        {1: mid_spec}, work_x, work_z, rows_inv, cols_inv, take,
    )


def main_kernel(
    logit_ref, target_ref, even_ref, odd_ref, taps3, table_ref,
    early_spectra, own_cols, mid_spec, mid_fields, mid_total,
    out_ref,
    late_spectra, mask_spec, fields, total, slope, work_t, work_x, work_z, work_b, grad_spec,
):
    (
        taps_cols, taps_rows, mask_cols, rows_fwd, rows_inv, cols_inv, cols_fwd, grad_rows, grad_cols
    ) = table_views(table_ref)
    rows, cols = logit_ref.shape
    reach = SIZE - STEP
    half = reach // 2
    place = lax.axis_index("kern")
    band = lax.axis_index("tile")
    bands = lax.axis_size("tile")
    field_rows = rows + reach
    windows = field_rows // STEP
    outs = rows // STEP
    early = early_spectra.shape[0]
    late = taps3.shape[0]
    count = early + late
    pairs = count // 2
    spectra = [early_spectra.at[kernel] for kernel in range(early)]
    spectra += [late_spectra.at[kernel] for kernel in range(late)]

    even = lax.rem(band, 2) == 0
    above = jnp.where(even, odd_ref[...], even_ref[...])
    below = jnp.where(even, even_ref[...], odd_ref[...])
    lane = lax.broadcasted_iota(jnp.int32, (half, SIZE), 1)

    def second(block):
        outer = block[reach:reach + half]
        inner = pltpu.roll(block[0:reach], STEP, 1)
        return jnp.concatenate(
            [
                jnp.where(lane < STEP, inner[:half], pltpu.roll(outer, STEP, 1)),
                jnp.where(lane < STEP, inner[half:], outer),
            ],
            axis=0,
        )

    sides = (
        jnp.concatenate([above[0:reach], below[0:reach]], axis=0),
        jnp.concatenate([second(above), second(below)], axis=0),
    )
    last = windows - 1
    for side, window in enumerate(sides):
        mixed = right_dot(window, mask_cols)
        span = slice(side * SIZE, (side + 1) * SIZE)
        for half_at, part in enumerate(split(mixed)):
            for phase in range(2):
                cut = slice(phase * SIZE, (phase + 1) * SIZE)
                base = phase * SIZE
                work_x[0, 0, half_at, base:base + reach, span] = part[:reach, cut]
                work_x[0, last, half_at, base + STEP:base + SIZE, span] = part[reach:, cut]
    for half_at in range(2):
        for phase in range(2):
            base = phase * SIZE
            work_x[0, 0, half_at, base + reach:base + SIZE] = own_cols[half_at, phase, 0:STEP]
            work_x[0, last, half_at, base:base + STEP] = own_cols[half_at, phase, rows - STEP:]
    for index in (0, last):
        mask_spec[index] = left_dot(rows_fwd, (work_x[0, index, 0], work_x[0, index, 1]))

    all_spectra([taps3[kernel] for kernel in range(late)], work_t, taps_cols, taps_rows, late_spectra)

    total[0:STEP] = jnp.zeros((STEP, 2 * SIZE), F32)
    total[STEP:2 * STEP] = mid_total[...]
    total[2 * STEP:] = jnp.zeros((STEP, 2 * SIZE), F32)

    def take(kernel, index, pair):
        at_rows = slice(index * STEP, (index + 1) * STEP)
        for side, piece in enumerate(pair):
            cut = slice(side * SIZE, (side + 1) * SIZE)
            fields[kernel, at_rows, cut] = piece
            total[at_rows, cut] += piece * piece

    all_fields(
        [(kernel, (0, 2) if kernel < early else (0, 1, 2)) for kernel in range(count)],
        spectra, {0: mask_spec.at[0], 1: mid_spec, 2: mask_spec.at[2]},
        work_x, work_z, rows_inv, cols_inv, take,
    )

    def field(kernel):
        if kernel >= early:
            return fields[kernel]
        return jnp.concatenate(
            [fields[kernel, 0:STEP], mid_fields[kernel], fields[kernel, 2 * STEP:]], axis=0
        )

    target_near = jnp.concatenate(
        [above[reach + half:], own_target(target_ref[...], place), below[reach + half:]], axis=0
    )
    start = place * STEP - half
    target_turned = pltpu.roll(target_near, STEP, 1)
    lane = lax.broadcasted_iota(jnp.int32, (field_rows, SIZE), 1)
    row = lax.broadcasted_iota(jnp.int32, (field_rows, SIZE), 0) + band * rows - half
    first = lane < STEP
    low_lane = lane & (STEP - 1)
    for side in range(2):
        cut = slice(side * SIZE, (side + 1) * SIZE)
        squares = total[:, cut]
        intensity = squares + pltpu.roll(squares, STEP, 1)
        if side == 0:
            wanted = jnp.where(first, target_near, target_turned)
        else:
            wanted = jnp.where(first, target_turned, target_near)
        printed = jax.nn.sigmoid(RESIST_SLOPE * (intensity - RESIST_LEVEL))
        at = low_lane + (start + side * STEP)
        valid = (at >= 0) & (at < cols) & (row >= 0) & (row < bands * rows)
        slope[:, cut] = jnp.where(
            valid, (2.0 * RESIST_SLOPE) * (printed - wanted) * printed * (1.0 - printed), 0.0
        )

    grad_spec[...] = jnp.zeros_like(grad_spec)

    def grad_cols_step(pair, member):
        buffer = pair % BUFFERS
        span = slice(member * SIZE, (member + 1) * SIZE)
        mixed = right_dot(slope[...] * field(2 * pair + member), cols_fwd)
        for half_at, part in enumerate(split(mixed)):
            for index in range(outs):
                at = slice(index * STEP, index * STEP + SIZE)
                work_b[buffer, index, half_at, 0:SIZE, span] = part[at, :SIZE]
                work_b[buffer, index, half_at, SIZE:, span] = part[at, SIZE:]

    def grad_rows_step(pair, index):
        buffer = pair % BUFFERS
        spec = left_dot(rows_fwd, (work_b[buffer, index, 0], work_b[buffer, index, 1]))
        cut = slice(index * SIZE, (index + 1) * SIZE)
        sum_re = grad_spec[0:SIZE, cut]
        sum_im = grad_spec[SIZE:, cut]
        for member in range(2):
            span = slice(member * SIZE, (member + 1) * SIZE)
            kern_re = spectra[2 * pair + member][0:SIZE]
            kern_im = spectra[2 * pair + member][SIZE:]
            spec_re = spec[0:SIZE, span]
            spec_im = spec[SIZE:, span]
            sum_re = sum_re + kern_re * spec_re + kern_im * spec_im
            sum_im = sum_im + kern_re * spec_im - kern_im * spec_re
        grad_spec[0:SIZE, cut] = sum_re
        grad_spec[SIZE:, cut] = sum_im

    for pair in range(pairs + 1):
        for part in range(2):
            if pair < pairs:
                grad_cols_step(pair, part)
            if pair > 0:
                for index in range(part, outs, 2):
                    grad_rows_step(pair - 1, index)

    halfway = left_dot(grad_rows, split(grad_spec[...]))
    stacked = jnp.concatenate(
        [
            jnp.concatenate(
                [
                    halfway[0:STEP, index * SIZE:(index + 1) * SIZE],
                    halfway[STEP:, index * SIZE:(index + 1) * SIZE],
                ],
                axis=1,
            )
            for index in range(outs)
        ],
        axis=0,
    )
    high, low = split(stacked)
    both = dot(high, grad_cols[:, :SIZE])
    gradient = both[:, :STEP] + (both[:, STEP:] + dot(low, grad_cols[:, :STEP]))
    mask_share = pltpu.roll(
        jax.nn.sigmoid(MASK_SLOPE * logit_ref[...]), lax.rem(cols - place * STEP, cols), 1
    )[:, :STEP]
    out_ref[...] = jnp.transpose(
        gradient * (2.0 * MASK_SLOPE) * mask_share * (1.0 - mask_share)
    )


def body(mask_logit, target, kern_real, kern_imag, kern_weight):
    rows, cols = mask_logit.shape
    local, tap_count, _ = kern_real.shape
    reach = tap_count - 1
    kern_size = lax.axis_size("kern")
    tile_size = lax.axis_size("tile")
    assert reach == SIZE - STEP and cols == STEP * kern_size and rows % STEP == 0
    assert kern_size == 4 and rows == SIZE
    half = reach // 2
    vmem = pl.BlockSpec(memory_space=pltpu.VMEM)
    smem = pl.BlockSpec(memory_space=pltpu.SMEM)


    even, odd, taps = pl.pallas_call(
        pack_kernel,
        out_shape=(
            jax.ShapeDtypeStruct((2 * reach, SIZE), F32),
            jax.ShapeDtypeStruct((2 * reach, SIZE), F32),
            jax.ShapeDtypeStruct((local, TAP_ROWS, SIZE), F32),
        ),
        in_specs=[smem] + [vmem] * 4,
        out_specs=(vmem,) * 3,
    )(kern_weight, mask_logit, target, kern_real, kern_imag)

    def swaps(first):
        return [p for i in range(first, tile_size - 1, 2) for p in ((i, i + 1), (i + 1, i))]

    def flipped(value, flip):
        return lax.ppermute(value, "kern", [(i, i ^ flip) for i in range(kern_size)])

    far = flipped(taps, 2)
    near = flipped(taps, 1)
    even = lax.ppermute(even, "tile", swaps(0))
    odd = lax.ppermute(odd, "tile", swaps(1))
    both = flipped(far, 1)

    table = pl.pallas_call(
        table_kernel,
        out_shape=jax.ShapeDtypeStruct((sum(TABLE_ROWS), 2 * SIZE), BF16),
        out_specs=vmem,
        compiler_params=pltpu.CompilerParams(vmem_limit_bytes=8 * 1024 * 1024),
        cost_estimate=pl.CostEstimate(flops=2 * 10**9, bytes_accessed=5 * 10**6, transcendentals=0),
    )()
    field_rows = rows + reach
    windows = field_rows // STEP
    outs = rows // STEP
    count = local * kern_size
    early = count - local
    local_out = pl.pallas_call(
        local_kernel,
        out_shape=(
            jax.ShapeDtypeStruct((early, 2 * SIZE, SIZE), F32),
            jax.ShapeDtypeStruct((2, 2, rows, 2 * SIZE), BF16),
            jax.ShapeDtypeStruct((2 * SIZE, 2 * SIZE), F32),
            jax.ShapeDtypeStruct((early, STEP, 2 * SIZE), F32),
            jax.ShapeDtypeStruct((STEP, 2 * SIZE), F32),
        ),
        in_specs=[vmem] * 5,
        out_specs=(vmem,) * 5,
        scratch_shapes=[
            pltpu.VMEM((early * TAP_ROWS, 4 * SIZE), BF16),
            pltpu.VMEM((BUFFERS, 1, 2, 2 * SIZE, 2 * SIZE), BF16),
            pltpu.VMEM((BUFFERS, 2, 2 * STEP, 2 * SIZE), BF16),
        ],
        compiler_params=pltpu.CompilerParams(vmem_limit_bytes=16 * 1024 * 1024),
        cost_estimate=pl.CostEstimate(flops=4 * 10**9, bytes_accessed=5 * 10**6, transcendentals=0),
    )(mask_logit, taps, near, far, table)
    result = pl.pallas_call(
        main_kernel,
        out_shape=jax.ShapeDtypeStruct((STEP, rows), F32),
        in_specs=[vmem] * (6 + len(local_out)),
        out_specs=vmem,
        scratch_shapes=[
            pltpu.VMEM((local, 2 * SIZE, SIZE), F32),
            pltpu.VMEM((windows, 2 * SIZE, 2 * SIZE), F32),
            pltpu.VMEM((count, field_rows, 2 * SIZE), F32),
            pltpu.VMEM((field_rows, 2 * SIZE), F32),
            pltpu.VMEM((field_rows, 2 * SIZE), F32),
            pltpu.VMEM((local * TAP_ROWS, 4 * SIZE), BF16),
            pltpu.VMEM((BUFFERS, windows, 2, 2 * SIZE, 2 * SIZE), BF16),
            pltpu.VMEM((BUFFERS, 2, 2 * windows * STEP, 2 * SIZE), BF16),
            pltpu.VMEM((BUFFERS, outs, 2, 2 * SIZE, 2 * SIZE), BF16),
            pltpu.VMEM((2 * SIZE, outs * SIZE), F32),
        ],
        compiler_params=pltpu.CompilerParams(vmem_limit_bytes=24 * 1024 * 1024),
    )(mask_logit, target, even, odd, both, table, *local_out)
    return jnp.transpose(result)


def solution(mesh):
    in_specs = (
        P("tile", None),
        P("tile", None),
        P("kern", None, None),
        P("kern", None, None),
        P("kern"),
    )
    out_specs = P("tile", "kern")
    return jax.shard_map(body, mesh=mesh, in_specs=in_specs, out_specs=out_specs, check_vma=False)
```

```python
import functools
import math

import jax
import jax.numpy as jnp
from jax import lax
from jax.experimental import pallas as pl
from jax.experimental.pallas import tpu as pltpu
from jax.sharding import PartitionSpec as P

MASK_SLOPE = 3.0
RESIST_SLOPE = 6.0
RESIST_LEVEL = 1.0

STEP = 64
SIZE = 128
TAP_ROWS = 72

F32 = jnp.float32
BF16 = jnp.bfloat16
TABLE_ROWS = (384, 512, 256, 512, 256, 256, 512, 256, 256)
BUFFERS = 6


def table_views(ref):
    views, at = [], 0
    for rows in TABLE_ROWS:
        views.append(ref.at[at:at + rows])
        at += rows
    return views


def split(value):
    high = value.astype(BF16)
    return high, (value - high.astype(F32)).astype(BF16)


def dot(left, right):
    return jnp.dot(left, right, preferred_element_type=F32)


def own_window(logit, place):
    cols = logit.shape[1]
    start = (place - 1) * STEP
    turned = pltpu.roll(jax.nn.sigmoid(MASK_SLOPE * logit), lax.rem(2 * cols - start, cols), 1)
    at = lax.broadcasted_iota(jnp.int32, logit.shape, 1) + start
    return jnp.where((at >= 0) & (at < cols), turned, 0.0)


def own_target(target, place):
    cols = target.shape[1]
    start = place * STEP - STEP // 2
    return pltpu.roll(target.astype(F32), lax.rem(2 * cols - start, cols), 1)[:, :SIZE]


def left_dot(table, value):
    rows = table.shape[0] // 2
    high, low = value
    both = dot(table[...], high)
    return both[:rows] + (both[rows:] + dot(table[0:rows], low))


def unit_waves():
    row = lax.broadcasted_iota(jnp.int32, (SIZE, SIZE), 0)
    col = lax.broadcasted_iota(jnp.int32, (SIZE, SIZE), 1)
    phase = (row * col) & (SIZE - 1)
    quarter = (phase + SIZE // 8) >> (SIZE.bit_length() - 3)
    rest = phase - quarter * (SIZE // 4)
    angle = rest.astype(F32) * (2.0 * math.pi / SIZE)
    square = angle * angle
    sin_near = cos_near = jnp.ones_like(angle)
    for step in (8, 6, 4, 2):
        sin_near = 1.0 - square * (1.0 / (step * (step + 1))) * sin_near
    for step in (10, 8, 6, 4, 2):
        cos_near = 1.0 - square * (1.0 / (step * (step - 1))) * cos_near
    sin_near = sin_near * angle
    turned = (quarter & 1) == 1
    cos_all = jnp.where(turned, -sin_near, cos_near)
    sin_all = jnp.where(turned, cos_near, sin_near)
    flip = (quarter & 2) == 2
    return jnp.where(flip, -cos_all, cos_all), jnp.where(flip, -sin_all, sin_all)


def table_kernel(table_ref):
    (
        taps_cols, taps_rows, mask_cols, rows_fwd, rows_inv, cols_inv, cols_fwd, grad_rows, grad_cols
    ) = table_views(table_ref)
    cos, sin = unit_waves()
    lane = lax.broadcasted_iota(jnp.int32, (SIZE, SIZE), 1)
    row = lax.broadcasted_iota(jnp.int32, (SIZE, SIZE), 0)
    left = lane < STEP
    scale = 1.0 / SIZE
    near, far = slice(0, STEP), slice(STEP, SIZE)

    def put(ref, blocks):
        rows = ref.shape[0] // 2
        at = 0
        for first, second in blocks:
            for column, value in enumerate((first, second)):
                for base, part in zip((0, rows), split(value)):
                    span = slice(column * SIZE, (column + 1) * SIZE)
                    ref[base + at:base + at + value.shape[0], span] = part
            at += first.shape[0]

    put(taps_cols.at[0:2 * SIZE], ((cos[near], sin[near]), (-sin[near], cos[near])))
    sign = (1 - 2 * (lane & 1)).astype(F32)
    even = (row & 1) == 0
    taps_cols[2 * SIZE:, :SIZE] = jnp.where(even, sign, 0.0).astype(BF16)
    taps_cols[2 * SIZE:, SIZE:] = jnp.where(even, 0.0, sign).astype(BF16)
    live = lane < SIZE - STEP + 1
    held = [[part.astype(F32) for part in split(jnp.where(live, wave, 0.0))] for wave in (cos, sin)]
    (cos_high, cos_low), (sin_high, sin_low) = held
    for phase, parts in enumerate((
        (cos_high, -sin_high, cos_high, -sin_high, cos_low, -sin_low),
        (sin_high, cos_high, sin_high, cos_high, sin_low, cos_low),
    )):
        for block in range(4):
            value = jnp.zeros((SIZE, SIZE), F32)
            for index, part in enumerate(parts):
                shift = index * TAP_ROWS - block * SIZE
                if -TAP_ROWS < shift < SIZE:
                    moved = pltpu.roll(part, shift % SIZE, 1) if shift % SIZE else part
                    value = jnp.where((lane >= shift) & (lane < shift + TAP_ROWS), moved, value)
            base = (block // 2) * 2 * SIZE + phase * SIZE
            span = slice((block % 2) * SIZE, (block % 2 + 1) * SIZE)
            taps_rows[base:base + SIZE, span] = value.astype(BF16)
    put(mask_cols, ((cos, -sin),))
    put(rows_fwd, ((cos, sin), (-sin, cos)))
    cos_s, sin_s = cos * scale, sin * scale
    put(rows_inv, ((cos_s[near], -sin_s[near]), (sin_s[near], cos_s[near])))
    cos_r, sin_r = pltpu.roll(cos_s, STEP, 1), pltpu.roll(sin_s, STEP, 1)
    for phase, value in enumerate((
        jnp.where(left, cos_s, sin_r), jnp.where(left, -sin_s, cos_r)
    )):
        for column, part in enumerate(split(value)):
            span = slice(column * SIZE, (column + 1) * SIZE)
            cols_inv[phase * SIZE:(phase + 1) * SIZE, span] = part
    put(cols_fwd, [
        pair for half in (near, far) for pair in ((cos[half], -sin[half]), (sin[half], cos[half]))
    ])
    put(grad_rows, ((cos_s[far], -sin_s[far]), (sin_s[far], cos_s[far])))
    for phase, (moved, value) in enumerate(((cos_r, cos_s), (-sin_r, -sin_s))):
        both = jnp.where(left, split(moved)[0].astype(F32), split(value)[1].astype(F32))
        grad_cols[phase * SIZE:(phase + 1) * SIZE, :SIZE] = both.astype(BF16)
        grad_cols[phase * SIZE:(phase + 1) * SIZE, SIZE:] = jnp.zeros((SIZE, SIZE), BF16)


def pack_kernel(weight_ref, logit_ref, target_ref, real_ref, imag_ref, even_ref, odd_ref, taps_ref):
    rows = logit_ref.shape[0]
    reach = SIZE - STEP
    half = reach // 2
    place = lax.axis_index("kern")
    to_next = lax.rem(lax.axis_index("tile"), 2) == 0
    window = own_window(logit_ref[...], place)
    wanted = own_target(target_ref[...], place)

    def packed(ref, near, near_target):
        ref[0:reach] = near[:, :SIZE]
        ref[reach:reach + half, :STEP] = near[:half, SIZE:SIZE + STEP]
        ref[reach:reach + half, STEP:] = near[half:, SIZE:SIZE + STEP]
        ref[reach + half:] = near_target

    top = window[0:reach]
    bottom = window[rows - reach:]
    top_target = wanted[0:half]
    bottom_target = wanted[rows - half:]
    packed(even_ref, jnp.where(to_next, bottom, top), jnp.where(to_next, bottom_target, top_target))
    packed(odd_ref, jnp.where(to_next, top, bottom), jnp.where(to_next, top_target, bottom_target))

    count = real_ref.shape[1]
    sublane = lax.broadcasted_iota(jnp.int32, (count, count), 0)
    lane = lax.broadcasted_iota(jnp.int32, (count, count), 1)
    taps_ref[...] = jnp.zeros_like(taps_ref)
    for kernel in range(real_ref.shape[0]):
        root = jnp.sqrt(jnp.full((1, count), weight_ref[kernel], F32))
        for part, ref in enumerate((real_ref, imag_ref)):
            taps = ref[kernel] * root
            taps_ref[kernel, 0:count, part * STEP:(part + 1) * STEP] = taps[:, :STEP]
            last = jnp.where(sublane == lane, taps[:, STEP:STEP + 1], 0.0)
            taps_ref[kernel, count + part:count + part + 1, 0:count] = jnp.sum(
                last, axis=0, keepdims=True
            )


def right_dot(value, table):
    high, low = split(value)
    rows = table.shape[0] // 2
    whole = jnp.concatenate([table[0:rows], table[0:rows], table[rows:]], axis=0)
    return dot(jnp.concatenate([high, low, high], axis=1), whole)


def tap_columns(blocks, work_t, taps_cols):
    tap_rows = blocks[0].shape[0]
    tap_count = SIZE - STEP + 1
    ends = [block[tap_count:tap_count + 2] for block in blocks]
    ends.append(jnp.zeros((STEP - 2 * len(blocks), SIZE), F32))
    ends = jnp.concatenate(ends, axis=0)
    turned = jnp.transpose(jnp.concatenate([ends, ends], axis=0))[:tap_rows]
    lane = lax.broadcasted_iota(jnp.int32, turned.shape, 1)
    coarse = turned.astype(BF16).astype(F32)
    turned = jnp.where(lane < STEP, coarse, turned - coarse)
    owner = (lane & (STEP - 1)) >> 1
    for index, block in enumerate(blocks):
        part = slice(index * tap_rows, (index + 1) * tap_rows)
        high, low = split(block)
        work_t[part, 0:128] = high
        work_t[part, 128:256] = low
        work_t[part, 256:384] = high
        work_t[part, 384:512] = jnp.where(owner == index, turned, 0.0).astype(BF16)
    table = [taps_cols[at * SIZE:(at + 1) * SIZE] for at in (0, 0, 1, 2)]
    return dot(work_t[0:len(blocks) * tap_rows], jnp.concatenate(table, axis=0))


def tap_spectra(mixed, indices, taps_rows, store):
    columns = []
    for index in indices:
        part = slice(index * TAP_ROWS, (index + 1) * TAP_ROWS)
        columns.append(jnp.concatenate([mixed[part, :SIZE], mixed[part, SIZE:]], axis=0))
    high, low = split(jnp.concatenate(columns, axis=1))
    wide = jnp.concatenate([taps_rows[0:2 * SIZE], taps_rows[2 * SIZE:]], axis=1)
    spectra = dot(wide[:, :6 * TAP_ROWS], jnp.concatenate([high, low, high], axis=0))
    for place, index in enumerate(indices):
        store(index, spectra[:, place * SIZE:(place + 1) * SIZE])


def field_products(spectrum, mask_spec, work):
    for side in range(2):
        cut = slice(side * SIZE, (side + 1) * SIZE)
        kern_re = spectrum[0:SIZE]
        kern_im = spectrum[SIZE:]
        mask_re = mask_spec[0:SIZE, cut]
        mask_im = mask_spec[SIZE:, cut]
        high, low = split(mask_re * kern_re - mask_im * kern_im)
        work[0, 0:SIZE, cut] = high
        work[1, 0:SIZE, cut] = low
        high, low = split(mask_re * kern_im + mask_im * kern_re)
        work[0, SIZE:, cut] = high
        work[1, SIZE:, cut] = low


def field_rows_step(work, work_z, index, rows_inv):
    high, low = split(left_dot(rows_inv, (work[0], work[1])))
    for side in range(2):
        cut = slice(side * SIZE, (side + 1) * SIZE)
        base = (index * 2 + side) * STEP
        at = slice(base, base + STEP)
        work_z[0, at, 0:SIZE] = high[0:STEP, cut]
        work_z[0, at, SIZE:] = high[STEP:, cut]
        work_z[1, at, 0:SIZE] = low[0:STEP, cut]
        work_z[1, at, SIZE:] = low[STEP:, cut]


def field_cols_step(work_z, windows, cols_inv):
    pieces = windows * 2
    major = dot(work_z[0, 0:pieces * STEP], cols_inv[...])
    minor = dot(work_z[1, 0:pieces * STEP], cols_inv[:, 0:SIZE])
    result = major[:, 0:SIZE] + (major[:, SIZE:] + minor)
    return [
        [result[(index * 2 + side) * STEP:(index * 2 + side + 1) * STEP] for side in range(2)]
        for index in range(windows)
    ]


def all_spectra(blocks, work_t, taps_cols, taps_rows, out):
    mixed = tap_columns(blocks, work_t, taps_cols)

    def store(index, value):
        out[index] = value

    for first in range(0, len(blocks), 2):
        tap_spectra(mixed, range(first, min(first + 2, len(blocks))), taps_rows, store)


def all_fields(todo, spectra, mask_specs, work_x, work_z, rows_inv, cols_inv, take):
    def products(at, slot):
        kernel, windows = todo[at]
        field_products(
            spectra[kernel], mask_specs[windows[slot]], work_x.at[at % BUFFERS, slot]
        )

    for slot in range(len(todo[0][1])):
        products(0, slot)
    for at in range(len(todo) + 1):
        later = len(todo[at + 1][1]) if at + 1 < len(todo) else 0
        now = len(todo[at][1]) if at < len(todo) else 0
        for slot in range(max(later, now)):
            if slot < later:
                products(at + 1, slot)
            if slot < now:
                buffer = at % BUFFERS
                field_rows_step(work_x.at[buffer, slot], work_z.at[buffer], slot, rows_inv)
        if at > 0:
            kernel, windows = todo[at - 1]
            pieces = field_cols_step(work_z.at[(at - 1) % BUFFERS], len(windows), cols_inv)
            for index, pair in zip(windows, pieces):
                take(kernel, index, pair)


def local_kernel(
    logit_ref, taps0, taps1, taps2, table_ref,
    spectra, own_cols, mid_spec, mid_fields, mid_total,
    work_t, work_x, work_z,
):
    taps_cols, taps_rows, mask_cols, rows_fwd, rows_inv, cols_inv = table_views(table_ref)[:6]
    rows, cols = logit_ref.shape
    own = own_window(logit_ref[...], lax.axis_index("kern"))
    for side in range(2):
        window = own[:, :SIZE] if side == 0 else pltpu.roll(own, cols - STEP, 1)[:, :SIZE]
        mixed = right_dot(window, mask_cols)
        span = slice(side * SIZE, (side + 1) * SIZE)
        for half_at, part in enumerate(split(mixed)):
            own_cols[half_at, 0, :, span] = part[:, :SIZE]
            own_cols[half_at, 1, :, span] = part[:, SIZE:]
    mid_spec[...] = left_dot(
        rows_fwd,
        (own_cols[0].reshape(2 * rows, 2 * SIZE), own_cols[1].reshape(2 * rows, 2 * SIZE)),
    )
    blocks = [ref[kernel] for ref in (taps0, taps1, taps2) for kernel in range(ref.shape[0])]
    all_spectra(blocks, work_t, taps_cols, taps_rows, spectra)
    mid_total[...] = jnp.zeros_like(mid_total)

    def take(kernel, index, pair):
        for side, piece in enumerate(pair):
            cut = slice(side * SIZE, (side + 1) * SIZE)
            mid_fields[kernel, :, cut] = piece
            mid_total[:, cut] += piece * piece

    all_fields(
        [(kernel, (1,)) for kernel in range(len(blocks))],
        [spectra.at[kernel] for kernel in range(len(blocks))],
        {1: mid_spec}, work_x, work_z, rows_inv, cols_inv, take,
    )


def main_kernel(
    logit_ref, target_ref, even_ref, odd_ref, taps3, table_ref,
    early_spectra, own_cols, mid_spec, mid_fields, mid_total,
    out_ref,
    late_spectra, mask_spec, fields, total, slope, work_t, work_m, work_x, work_z, work_b, grad_spec,
):
    (
        taps_cols, taps_rows, mask_cols, rows_fwd, rows_inv, cols_inv, cols_fwd, grad_rows, grad_cols
    ) = table_views(table_ref)
    rows, cols = logit_ref.shape
    reach = SIZE - STEP
    half = reach // 2
    place = lax.axis_index("kern")
    band = lax.axis_index("tile")
    bands = lax.axis_size("tile")
    field_rows = rows + reach
    windows = field_rows // STEP
    outs = rows // STEP
    early = early_spectra.shape[0]
    late = taps3.shape[0]
    count = early + late
    pairs = count // 2
    spectra = [early_spectra.at[kernel] for kernel in range(early)]
    spectra += [late_spectra.at[kernel] for kernel in range(late)]

    even = lax.rem(band, 2) == 0
    above = jnp.where(even, odd_ref[...], even_ref[...])
    below = jnp.where(even, even_ref[...], odd_ref[...])
    lane = lax.broadcasted_iota(jnp.int32, (half, SIZE), 1)

    def second(block):
        outer = block[reach:reach + half]
        inner = pltpu.roll(block[0:reach], STEP, 1)
        return jnp.concatenate(
            [
                jnp.where(lane < STEP, inner[:half], pltpu.roll(outer, STEP, 1)),
                jnp.where(lane < STEP, inner[half:], outer),
            ],
            axis=0,
        )

    sides = (
        jnp.concatenate([above[0:reach], below[0:reach]], axis=0),
        jnp.concatenate([second(above), second(below)], axis=0),
    )
    last = windows - 1
    for side, window in enumerate(sides):
        mixed = right_dot(window, mask_cols)
        span = slice(side * SIZE, (side + 1) * SIZE)
        for half_at, part in enumerate(split(mixed)):
            for phase in range(2):
                cut = slice(phase * SIZE, (phase + 1) * SIZE)
                base = phase * SIZE
                work_m[0, half_at, base:base + reach, span] = part[:reach, cut]
                work_m[last, half_at, base + STEP:base + SIZE, span] = part[reach:, cut]
    for half_at in range(2):
        for phase in range(2):
            base = phase * SIZE
            work_m[0, half_at, base + reach:base + SIZE] = own_cols[half_at, phase, 0:STEP]
            work_m[last, half_at, base:base + STEP] = own_cols[half_at, phase, rows - STEP:]
    for index in (0, last):
        mask_spec[index] = left_dot(rows_fwd, (work_m[index, 0], work_m[index, 1]))

    all_spectra([taps3[kernel] for kernel in range(late)], work_t, taps_cols, taps_rows, late_spectra)

    total[0:STEP] = jnp.zeros((STEP, 2 * SIZE), F32)
    total[STEP:2 * STEP] = mid_total[...]
    total[2 * STEP:] = jnp.zeros((STEP, 2 * SIZE), F32)

    def take(kernel, index, pair):
        at_rows = slice(index * STEP, (index + 1) * STEP)
        for side, piece in enumerate(pair):
            cut = slice(side * SIZE, (side + 1) * SIZE)
            fields[kernel, at_rows, cut] = piece
            total[at_rows, cut] += piece * piece

    all_fields(
        [(kernel, (0, 2) if kernel < early else (0, 1, 2)) for kernel in range(count)],
        spectra, {0: mask_spec.at[0], 1: mid_spec, 2: mask_spec.at[2]},
        work_x, work_z, rows_inv, cols_inv, take,
    )

    def field(kernel):
        if kernel >= early:
            return fields[kernel]
        return jnp.concatenate(
            [fields[kernel, 0:STEP], mid_fields[kernel], fields[kernel, 2 * STEP:]], axis=0
        )

    target_near = jnp.concatenate(
        [above[reach + half:], own_target(target_ref[...], place), below[reach + half:]], axis=0
    )
    start = place * STEP - half
    target_turned = pltpu.roll(target_near, STEP, 1)
    lane = lax.broadcasted_iota(jnp.int32, (field_rows, SIZE), 1)
    row = lax.broadcasted_iota(jnp.int32, (field_rows, SIZE), 0) + band * rows - half
    first = lane < STEP
    low_lane = lane & (STEP - 1)
    for side in range(2):
        cut = slice(side * SIZE, (side + 1) * SIZE)
        squares = total[:, cut]
        intensity = squares + pltpu.roll(squares, STEP, 1)
        if side == 0:
            wanted = jnp.where(first, target_near, target_turned)
        else:
            wanted = jnp.where(first, target_turned, target_near)
        printed = jax.nn.sigmoid(RESIST_SLOPE * (intensity - RESIST_LEVEL))
        at = low_lane + (start + side * STEP)
        valid = (at >= 0) & (at < cols) & (row >= 0) & (row < bands * rows)
        slope[:, cut] = jnp.where(
            valid, (2.0 * RESIST_SLOPE) * (printed - wanted) * printed * (1.0 - printed), 0.0
        )

    grad_spec[...] = jnp.zeros_like(grad_spec)

    def grad_cols_step(pair, member):
        buffer = pair % BUFFERS
        span = slice(member * SIZE, (member + 1) * SIZE)
        mixed = right_dot(slope[...] * field(2 * pair + member), cols_fwd)
        for half_at, part in enumerate(split(mixed)):
            for index in range(outs):
                at = slice(index * STEP, index * STEP + SIZE)
                work_b[buffer, index, half_at, 0:SIZE, span] = part[at, :SIZE]
                work_b[buffer, index, half_at, SIZE:, span] = part[at, SIZE:]

    def grad_rows_step(pair, index):
        buffer = pair % BUFFERS
        spec = left_dot(rows_fwd, (work_b[buffer, index, 0], work_b[buffer, index, 1]))
        cut = slice(index * SIZE, (index + 1) * SIZE)
        sum_re = grad_spec[0:SIZE, cut]
        sum_im = grad_spec[SIZE:, cut]
        for member in range(2):
            span = slice(member * SIZE, (member + 1) * SIZE)
            kern_re = spectra[2 * pair + member][0:SIZE]
            kern_im = spectra[2 * pair + member][SIZE:]
            spec_re = spec[0:SIZE, span]
            spec_im = spec[SIZE:, span]
            sum_re = sum_re + kern_re * spec_re + kern_im * spec_im
            sum_im = sum_im + kern_re * spec_im - kern_im * spec_re
        grad_spec[0:SIZE, cut] = sum_re
        grad_spec[SIZE:, cut] = sum_im

    for pair in range(pairs + 1):
        for part in range(2):
            if pair < pairs:
                grad_cols_step(pair, part)
            if pair > 0:
                for index in range(part, outs, 2):
                    grad_rows_step(pair - 1, index)

    halfway = left_dot(grad_rows, split(grad_spec[...]))
    stacked = jnp.concatenate(
        [
            jnp.concatenate(
                [
                    halfway[0:STEP, index * SIZE:(index + 1) * SIZE],
                    halfway[STEP:, index * SIZE:(index + 1) * SIZE],
                ],
                axis=1,
            )
            for index in range(outs)
        ],
        axis=0,
    )
    high, low = split(stacked)
    both = dot(high, grad_cols[:, :SIZE])
    gradient = both[:, :STEP] + (both[:, STEP:] + dot(low, grad_cols[:, :STEP]))
    mask_share = pltpu.roll(
        jax.nn.sigmoid(MASK_SLOPE * logit_ref[...]), lax.rem(cols - place * STEP, cols), 1
    )[:, :STEP]
    out_ref[...] = jnp.transpose(
        gradient * (2.0 * MASK_SLOPE) * mask_share * (1.0 - mask_share)
    )


def body(mask_logit, target, kern_real, kern_imag, kern_weight):
    rows, cols = mask_logit.shape
    local, tap_count, _ = kern_real.shape
    reach = tap_count - 1
    kern_size = lax.axis_size("kern")
    tile_size = lax.axis_size("tile")
    assert reach == SIZE - STEP and cols == STEP * kern_size and rows % STEP == 0
    assert kern_size == 4 and rows == SIZE
    half = reach // 2
    vmem = pl.BlockSpec(memory_space=pltpu.VMEM)
    smem = pl.BlockSpec(memory_space=pltpu.SMEM)


    even, odd, taps = pl.pallas_call(
        pack_kernel,
        out_shape=(
            jax.ShapeDtypeStruct((2 * reach, SIZE), F32),
            jax.ShapeDtypeStruct((2 * reach, SIZE), F32),
            jax.ShapeDtypeStruct((local, TAP_ROWS, SIZE), F32),
        ),
        in_specs=[smem] + [vmem] * 4,
        out_specs=(vmem,) * 3,
    )(kern_weight, mask_logit, target, kern_real, kern_imag)

    def swaps(first):
        return [p for i in range(first, tile_size - 1, 2) for p in ((i, i + 1), (i + 1, i))]

    def flipped(value, flip):
        return lax.ppermute(value, "kern", [(i, i ^ flip) for i in range(kern_size)])

    far = flipped(taps, 2)
    near = flipped(taps, 1)
    even = lax.ppermute(even, "tile", swaps(0))
    odd = lax.ppermute(odd, "tile", swaps(1))
    both = flipped(far, 1)

    table = pl.pallas_call(
        table_kernel,
        out_shape=jax.ShapeDtypeStruct((sum(TABLE_ROWS), 2 * SIZE), BF16),
        out_specs=vmem,
        compiler_params=pltpu.CompilerParams(vmem_limit_bytes=8 * 1024 * 1024),
        cost_estimate=pl.CostEstimate(flops=2 * 10**9, bytes_accessed=5 * 10**6, transcendentals=0),
    )()
    field_rows = rows + reach
    windows = field_rows // STEP
    outs = rows // STEP
    count = local * kern_size
    early = count - local
    local_out = pl.pallas_call(
        local_kernel,
        out_shape=(
            jax.ShapeDtypeStruct((early, 2 * SIZE, SIZE), F32),
            jax.ShapeDtypeStruct((2, 2, rows, 2 * SIZE), BF16),
            jax.ShapeDtypeStruct((2 * SIZE, 2 * SIZE), F32),
            jax.ShapeDtypeStruct((early, STEP, 2 * SIZE), F32),
            jax.ShapeDtypeStruct((STEP, 2 * SIZE), F32),
        ),
        in_specs=[vmem] * 5,
        out_specs=(vmem,) * 5,
        scratch_shapes=[
            pltpu.VMEM((early * TAP_ROWS, 4 * SIZE), BF16),
            pltpu.VMEM((BUFFERS, 1, 2, 2 * SIZE, 2 * SIZE), BF16),
            pltpu.VMEM((BUFFERS, 2, 2 * STEP, 2 * SIZE), BF16),
        ],
        compiler_params=pltpu.CompilerParams(vmem_limit_bytes=16 * 1024 * 1024),
        cost_estimate=pl.CostEstimate(flops=4 * 10**9, bytes_accessed=5 * 10**6, transcendentals=0),
    )(mask_logit, taps, near, far, table)
    result = pl.pallas_call(
        main_kernel,
        out_shape=jax.ShapeDtypeStruct((STEP, rows), F32),
        in_specs=[vmem] * (6 + len(local_out)),
        out_specs=vmem,
        scratch_shapes=[
            pltpu.VMEM((local, 2 * SIZE, SIZE), F32),
            pltpu.VMEM((windows, 2 * SIZE, 2 * SIZE), F32),
            pltpu.VMEM((count, field_rows, 2 * SIZE), F32),
            pltpu.VMEM((field_rows, 2 * SIZE), F32),
            pltpu.VMEM((field_rows, 2 * SIZE), F32),
            pltpu.VMEM((local * TAP_ROWS, 4 * SIZE), BF16),
            pltpu.VMEM((windows, 2, 2 * SIZE, 2 * SIZE), BF16),
            pltpu.VMEM((BUFFERS, windows, 2, 2 * SIZE, 2 * SIZE), BF16),
            pltpu.VMEM((BUFFERS, 2, 2 * windows * STEP, 2 * SIZE), BF16),
            pltpu.VMEM((BUFFERS, outs, 2, 2 * SIZE, 2 * SIZE), BF16),
            pltpu.VMEM((2 * SIZE, outs * SIZE), F32),
        ],
        compiler_params=pltpu.CompilerParams(vmem_limit_bytes=28 * 1024 * 1024),
    )(mask_logit, target, even, odd, both, table, *local_out)
    return jnp.transpose(result)


def solution(mesh):
    in_specs = (
        P("tile", None),
        P("tile", None),
        P("kern", None, None),
        P("kern", None, None),
        P("kern"),
    )
    out_specs = P("tile", "kern")
    return jax.shard_map(body, mesh=mesh, in_specs=in_specs, out_specs=out_specs, check_vma=False)
```

```python
import functools
import math

import jax
import jax.numpy as jnp
from jax import lax
from jax.experimental import pallas as pl
from jax.experimental.pallas import tpu as pltpu
from jax.sharding import PartitionSpec as P

MASK_SLOPE = 3.0
RESIST_SLOPE = 6.0
RESIST_LEVEL = 1.0

STEP = 64
SIZE = 128
TAP_ROWS = 72

F32 = jnp.float32
BF16 = jnp.bfloat16
TABLE_ROWS = (384, 512, 256, 512, 256, 256, 512, 256, 256)
BUFFERS = 3


def table_views(ref):
    views, at = [], 0
    for rows in TABLE_ROWS:
        views.append(ref.at[at:at + rows])
        at += rows
    return views


def split(value):
    high = value.astype(BF16)
    return high, (value - high.astype(F32)).astype(BF16)


def dot(left, right):
    return jnp.dot(left, right, preferred_element_type=F32)


def own_window(logit, place):
    cols = logit.shape[1]
    start = (place - 1) * STEP
    turned = pltpu.roll(jax.nn.sigmoid(MASK_SLOPE * logit), lax.rem(2 * cols - start, cols), 1)
    at = lax.broadcasted_iota(jnp.int32, logit.shape, 1) + start
    return jnp.where((at >= 0) & (at < cols), turned, 0.0)


def own_target(target, place):
    cols = target.shape[1]
    start = place * STEP - STEP // 2
    return pltpu.roll(target.astype(F32), lax.rem(2 * cols - start, cols), 1)[:, :SIZE]


def left_dot(table, value):
    rows = table.shape[0] // 2
    high, low = value
    both = dot(table[...], high)
    return both[:rows] + (both[rows:] + dot(table[0:rows], low))


def unit_waves():
    row = lax.broadcasted_iota(jnp.int32, (SIZE, SIZE), 0)
    col = lax.broadcasted_iota(jnp.int32, (SIZE, SIZE), 1)
    phase = (row * col) & (SIZE - 1)
    quarter = (phase + SIZE // 8) >> (SIZE.bit_length() - 3)
    rest = phase - quarter * (SIZE // 4)
    angle = rest.astype(F32) * (2.0 * math.pi / SIZE)
    square = angle * angle
    sin_near = cos_near = jnp.ones_like(angle)
    for step in (8, 6, 4, 2):
        sin_near = 1.0 - square * (1.0 / (step * (step + 1))) * sin_near
    for step in (10, 8, 6, 4, 2):
        cos_near = 1.0 - square * (1.0 / (step * (step - 1))) * cos_near
    sin_near = sin_near * angle
    turned = (quarter & 1) == 1
    cos_all = jnp.where(turned, -sin_near, cos_near)
    sin_all = jnp.where(turned, cos_near, sin_near)
    flip = (quarter & 2) == 2
    return jnp.where(flip, -cos_all, cos_all), jnp.where(flip, -sin_all, sin_all)


def table_kernel(table_ref):
    (
        taps_cols, taps_rows, mask_cols, rows_fwd, rows_inv, cols_inv, cols_fwd, grad_rows, grad_cols
    ) = table_views(table_ref)
    cos, sin = unit_waves()
    lane = lax.broadcasted_iota(jnp.int32, (SIZE, SIZE), 1)
    row = lax.broadcasted_iota(jnp.int32, (SIZE, SIZE), 0)
    left = lane < STEP
    scale = 1.0 / SIZE
    near, far = slice(0, STEP), slice(STEP, SIZE)

    def put(ref, blocks):
        rows = ref.shape[0] // 2
        at = 0
        for first, second in blocks:
            for column, value in enumerate((first, second)):
                for base, part in zip((0, rows), split(value)):
                    span = slice(column * SIZE, (column + 1) * SIZE)
                    ref[base + at:base + at + value.shape[0], span] = part
            at += first.shape[0]

    put(taps_cols.at[0:2 * SIZE], ((cos[near], sin[near]), (-sin[near], cos[near])))
    sign = (1 - 2 * (lane & 1)).astype(F32)
    even = (row & 1) == 0
    taps_cols[2 * SIZE:, :SIZE] = jnp.where(even, sign, 0.0).astype(BF16)
    taps_cols[2 * SIZE:, SIZE:] = jnp.where(even, 0.0, sign).astype(BF16)
    live = lane < SIZE - STEP + 1
    held = [[part.astype(F32) for part in split(jnp.where(live, wave, 0.0))] for wave in (cos, sin)]
    (cos_high, cos_low), (sin_high, sin_low) = held
    for phase, parts in enumerate((
        (cos_high, -sin_high, cos_high, -sin_high, cos_low, -sin_low),
        (sin_high, cos_high, sin_high, cos_high, sin_low, cos_low),
    )):
        for block in range(4):
            value = jnp.zeros((SIZE, SIZE), F32)
            for index, part in enumerate(parts):
                shift = index * TAP_ROWS - block * SIZE
                if -TAP_ROWS < shift < SIZE:
                    moved = pltpu.roll(part, shift % SIZE, 1) if shift % SIZE else part
                    value = jnp.where((lane >= shift) & (lane < shift + TAP_ROWS), moved, value)
            base = (block // 2) * 2 * SIZE + phase * SIZE
            span = slice((block % 2) * SIZE, (block % 2 + 1) * SIZE)
            taps_rows[base:base + SIZE, span] = value.astype(BF16)
    put(mask_cols, ((cos, -sin),))
    put(rows_fwd, ((cos, sin), (-sin, cos)))
    cos_s, sin_s = cos * scale, sin * scale
    put(rows_inv, ((cos_s[near], -sin_s[near]), (sin_s[near], cos_s[near])))
    cos_r, sin_r = pltpu.roll(cos_s, STEP, 1), pltpu.roll(sin_s, STEP, 1)
    for phase, value in enumerate((
        jnp.where(left, cos_s, sin_r), jnp.where(left, -sin_s, cos_r)
    )):
        for column, part in enumerate(split(value)):
            span = slice(column * SIZE, (column + 1) * SIZE)
            cols_inv[phase * SIZE:(phase + 1) * SIZE, span] = part
    put(cols_fwd, [
        pair for half in (near, far) for pair in ((cos[half], -sin[half]), (sin[half], cos[half]))
    ])
    put(grad_rows, ((cos_s[far], -sin_s[far]), (sin_s[far], cos_s[far])))
    for phase, (moved, value) in enumerate(((cos_r, cos_s), (-sin_r, -sin_s))):
        both = jnp.where(left, split(moved)[0].astype(F32), split(value)[1].astype(F32))
        grad_cols[phase * SIZE:(phase + 1) * SIZE, :SIZE] = both.astype(BF16)
        grad_cols[phase * SIZE:(phase + 1) * SIZE, SIZE:] = jnp.zeros((SIZE, SIZE), BF16)


def pack_kernel(weight_ref, logit_ref, target_ref, real_ref, imag_ref, even_ref, odd_ref, taps_ref):
    rows = logit_ref.shape[0]
    reach = SIZE - STEP
    half = reach // 2
    place = lax.axis_index("kern")
    to_next = lax.rem(lax.axis_index("tile"), 2) == 0
    window = own_window(logit_ref[...], place)
    wanted = own_target(target_ref[...], place)

    def packed(ref, near, near_target):
        ref[0:reach] = near[:, :SIZE]
        ref[reach:reach + half, :STEP] = near[:half, SIZE:SIZE + STEP]
        ref[reach:reach + half, STEP:] = near[half:, SIZE:SIZE + STEP]
        ref[reach + half:] = near_target

    top = window[0:reach]
    bottom = window[rows - reach:]
    top_target = wanted[0:half]
    bottom_target = wanted[rows - half:]
    packed(even_ref, jnp.where(to_next, bottom, top), jnp.where(to_next, bottom_target, top_target))
    packed(odd_ref, jnp.where(to_next, top, bottom), jnp.where(to_next, top_target, bottom_target))

    count = real_ref.shape[1]
    sublane = lax.broadcasted_iota(jnp.int32, (count, count), 0)
    lane = lax.broadcasted_iota(jnp.int32, (count, count), 1)
    taps_ref[...] = jnp.zeros_like(taps_ref)
    for kernel in range(real_ref.shape[0]):
        root = jnp.sqrt(jnp.full((1, count), weight_ref[kernel], F32))
        for part, ref in enumerate((real_ref, imag_ref)):
            taps = ref[kernel] * root
            taps_ref[kernel, 0:count, part * STEP:(part + 1) * STEP] = taps[:, :STEP]
            last = jnp.where(sublane == lane, taps[:, STEP:STEP + 1], 0.0)
            taps_ref[kernel, count + part:count + part + 1, 0:count] = jnp.sum(
                last, axis=0, keepdims=True
            )


def right_dot(value, table):
    high, low = split(value)
    rows = table.shape[0] // 2
    whole = jnp.concatenate([table[0:rows], table[0:rows], table[rows:]], axis=0)
    return dot(jnp.concatenate([high, low, high], axis=1), whole)


def tap_columns(blocks, work_t, taps_cols):
    tap_rows = blocks[0].shape[0]
    tap_count = SIZE - STEP + 1
    ends = [block[tap_count:tap_count + 2] for block in blocks]
    ends.append(jnp.zeros((STEP - 2 * len(blocks), SIZE), F32))
    ends = jnp.concatenate(ends, axis=0)
    turned = jnp.transpose(jnp.concatenate([ends, ends], axis=0))[:tap_rows]
    lane = lax.broadcasted_iota(jnp.int32, turned.shape, 1)
    coarse = turned.astype(BF16).astype(F32)
    turned = jnp.where(lane < STEP, coarse, turned - coarse)
    owner = (lane & (STEP - 1)) >> 1
    for index, block in enumerate(blocks):
        part = slice(index * tap_rows, (index + 1) * tap_rows)
        high, low = split(block)
        work_t[part, 0:128] = high
        work_t[part, 128:256] = low
        work_t[part, 256:384] = high
        work_t[part, 384:512] = jnp.where(owner == index, turned, 0.0).astype(BF16)
    table = [taps_cols[at * SIZE:(at + 1) * SIZE] for at in (0, 0, 1, 2)]
    return dot(work_t[0:len(blocks) * tap_rows], jnp.concatenate(table, axis=0))


def tap_spectra(mixed, indices, taps_rows, store):
    columns = []
    for index in indices:
        part = slice(index * TAP_ROWS, (index + 1) * TAP_ROWS)
        columns.append(jnp.concatenate([mixed[part, :SIZE], mixed[part, SIZE:]], axis=0))
    high, low = split(jnp.concatenate(columns, axis=1))
    wide = jnp.concatenate([taps_rows[0:2 * SIZE], taps_rows[2 * SIZE:]], axis=1)
    spectra = dot(wide[:, :6 * TAP_ROWS], jnp.concatenate([high, low, high], axis=0))
    for place, index in enumerate(indices):
        store(index, spectra[:, place * SIZE:(place + 1) * SIZE])


def field_products(spectrum, mask_spec, work):
    for side in range(2):
        cut = slice(side * SIZE, (side + 1) * SIZE)
        kern_re = spectrum[0:SIZE]
        kern_im = spectrum[SIZE:]
        mask_re = mask_spec[0:SIZE, cut]
        mask_im = mask_spec[SIZE:, cut]
        high, low = split(mask_re * kern_re - mask_im * kern_im)
        work[0, 0:SIZE, cut] = high
        work[1, 0:SIZE, cut] = low
        high, low = split(mask_re * kern_im + mask_im * kern_re)
        work[0, SIZE:, cut] = high
        work[1, SIZE:, cut] = low


def field_rows_store(result, work_z, index):
    high, low = split(result)
    for side in range(2):
        cut = slice(side * SIZE, (side + 1) * SIZE)
        base = (index * 2 + side) * STEP
        at = slice(base, base + STEP)
        work_z[0, at, 0:SIZE] = high[0:STEP, cut]
        work_z[0, at, SIZE:] = high[STEP:, cut]
        work_z[1, at, 0:SIZE] = low[0:STEP, cut]
        work_z[1, at, SIZE:] = low[STEP:, cut]


def staggered(units):
    waiting, active = list(units), []
    while waiting or active:
        if waiting:
            active.append(waiting.pop(0))
        active = [unit for unit in active if next(unit, True) is None]


def all_spectra(blocks, work_t, taps_cols, taps_rows, out):
    mixed = tap_columns(blocks, work_t, taps_cols)

    def store(index, value):
        out[index] = value

    for first in range(0, len(blocks), 2):
        tap_spectra(mixed, range(first, min(first + 2, len(blocks))), taps_rows, store)


def all_fields(todo, spectra, mask_specs, work_x, work_z, rows_inv, cols_inv, take):
    def unit(number, kernel, buffer, windows, slot):
        work, rows = work_x.at[number % BUFFERS], work_z.at[buffer]
        field_products(spectra[kernel], mask_specs[windows[slot]], work)
        yield
        result = left_dot(rows_inv, (work[0], work[1]))
        yield
        field_rows_store(result, rows, slot)
        if slot + 1 < len(windows):
            return
        yield
        pieces = len(windows) * 2 * STEP
        major = dot(rows[0, 0:pieces], cols_inv[...])
        minor = dot(rows[1, 0:pieces], cols_inv[:, 0:SIZE])
        yield
        result = major[:, 0:SIZE] + (major[:, SIZE:] + minor)
        for index, window in enumerate(windows):
            pair = [
                result[(index * 2 + side) * STEP:(index * 2 + side + 1) * STEP]
                for side in range(2)
            ]
            take(kernel, window, pair)

    units = []
    for at, (kernel, windows) in enumerate(todo):
        for slot in range(len(windows)):
            units.append(unit(len(units), kernel, at % BUFFERS, windows, slot))
    staggered(units)


def local_kernel(
    logit_ref, taps0, taps1, taps2, table_ref,
    spectra, own_cols, mid_spec, mid_fields, mid_total,
    work_t, work_x, work_z,
):
    taps_cols, taps_rows, mask_cols, rows_fwd, rows_inv, cols_inv = table_views(table_ref)[:6]
    rows, cols = logit_ref.shape
    own = own_window(logit_ref[...], lax.axis_index("kern"))
    for side in range(2):
        window = own[:, :SIZE] if side == 0 else pltpu.roll(own, cols - STEP, 1)[:, :SIZE]
        mixed = right_dot(window, mask_cols)
        span = slice(side * SIZE, (side + 1) * SIZE)
        for half_at, part in enumerate(split(mixed)):
            own_cols[half_at, 0, :, span] = part[:, :SIZE]
            own_cols[half_at, 1, :, span] = part[:, SIZE:]
    mid_spec[...] = left_dot(
        rows_fwd,
        (own_cols[0].reshape(2 * rows, 2 * SIZE), own_cols[1].reshape(2 * rows, 2 * SIZE)),
    )
    blocks = [ref[kernel] for ref in (taps0, taps1, taps2) for kernel in range(ref.shape[0])]
    all_spectra(blocks, work_t, taps_cols, taps_rows, spectra)
    mid_total[...] = jnp.zeros_like(mid_total)

    def take(kernel, index, pair):
        for side, piece in enumerate(pair):
            cut = slice(side * SIZE, (side + 1) * SIZE)
            mid_fields[kernel, :, cut] = piece
            mid_total[:, cut] += piece * piece

    all_fields(
        [(kernel, (1,)) for kernel in range(len(blocks))],
        [spectra.at[kernel] for kernel in range(len(blocks))],
        {1: mid_spec}, work_x, work_z, rows_inv, cols_inv, take,
    )


def main_kernel(
    logit_ref, target_ref, even_ref, odd_ref, taps3, table_ref,
    early_spectra, own_cols, mid_spec, mid_fields, mid_total,
    out_ref,
    late_spectra, mask_spec, fields, total, slope, work_t, work_x, work_z, work_b, grad_spec,
):
    (
        taps_cols, taps_rows, mask_cols, rows_fwd, rows_inv, cols_inv, cols_fwd, grad_rows, grad_cols
    ) = table_views(table_ref)
    rows, cols = logit_ref.shape
    reach = SIZE - STEP
    half = reach // 2
    place = lax.axis_index("kern")
    band = lax.axis_index("tile")
    bands = lax.axis_size("tile")
    field_rows = rows + reach
    windows = field_rows // STEP
    outs = rows // STEP
    early = early_spectra.shape[0]
    late = taps3.shape[0]
    count = early + late
    pairs = count // 2
    spectra = [early_spectra.at[kernel] for kernel in range(early)]
    spectra += [late_spectra.at[kernel] for kernel in range(late)]

    even = lax.rem(band, 2) == 0
    above = jnp.where(even, odd_ref[...], even_ref[...])
    below = jnp.where(even, even_ref[...], odd_ref[...])
    lane = lax.broadcasted_iota(jnp.int32, (half, SIZE), 1)

    def second(block):
        outer = block[reach:reach + half]
        inner = pltpu.roll(block[0:reach], STEP, 1)
        return jnp.concatenate(
            [
                jnp.where(lane < STEP, inner[:half], pltpu.roll(outer, STEP, 1)),
                jnp.where(lane < STEP, inner[half:], outer),
            ],
            axis=0,
        )

    sides = (
        jnp.concatenate([above[0:reach], below[0:reach]], axis=0),
        jnp.concatenate([second(above), second(below)], axis=0),
    )
    last = windows - 1
    for side, window in enumerate(sides):
        mixed = right_dot(window, mask_cols)
        span = slice(side * SIZE, (side + 1) * SIZE)
        for half_at, part in enumerate(split(mixed)):
            for phase in range(2):
                cut = slice(phase * SIZE, (phase + 1) * SIZE)
                base = phase * SIZE
                work_x[0, half_at, base:base + reach, span] = part[:reach, cut]
                work_x[last, half_at, base + STEP:base + SIZE, span] = part[reach:, cut]
    for half_at in range(2):
        for phase in range(2):
            base = phase * SIZE
            work_x[0, half_at, base + reach:base + SIZE] = own_cols[half_at, phase, 0:STEP]
            work_x[last, half_at, base:base + STEP] = own_cols[half_at, phase, rows - STEP:]
    for index in (0, last):
        mask_spec[index] = left_dot(rows_fwd, (work_x[index, 0], work_x[index, 1]))

    all_spectra([taps3[kernel] for kernel in range(late)], work_t, taps_cols, taps_rows, late_spectra)

    total[0:STEP] = jnp.zeros((STEP, 2 * SIZE), F32)
    total[STEP:2 * STEP] = mid_total[...]
    total[2 * STEP:] = jnp.zeros((STEP, 2 * SIZE), F32)

    def take(kernel, index, pair):
        at_rows = slice(index * STEP, (index + 1) * STEP)
        for side, piece in enumerate(pair):
            cut = slice(side * SIZE, (side + 1) * SIZE)
            fields[kernel, at_rows, cut] = piece
            total[at_rows, cut] += piece * piece

    all_fields(
        [(kernel, (0, 2) if kernel < early else (0, 1, 2)) for kernel in range(count)],
        spectra, {0: mask_spec.at[0], 1: mid_spec, 2: mask_spec.at[2]},
        work_x, work_z, rows_inv, cols_inv, take,
    )

    def field(kernel):
        if kernel >= early:
            return fields[kernel]
        return jnp.concatenate(
            [fields[kernel, 0:STEP], mid_fields[kernel], fields[kernel, 2 * STEP:]], axis=0
        )

    target_near = jnp.concatenate(
        [above[reach + half:], own_target(target_ref[...], place), below[reach + half:]], axis=0
    )
    start = place * STEP - half
    target_turned = pltpu.roll(target_near, STEP, 1)
    lane = lax.broadcasted_iota(jnp.int32, (field_rows, SIZE), 1)
    row = lax.broadcasted_iota(jnp.int32, (field_rows, SIZE), 0) + band * rows - half
    first = lane < STEP
    low_lane = lane & (STEP - 1)
    for side in range(2):
        cut = slice(side * SIZE, (side + 1) * SIZE)
        squares = total[:, cut]
        intensity = squares + pltpu.roll(squares, STEP, 1)
        if side == 0:
            wanted = jnp.where(first, target_near, target_turned)
        else:
            wanted = jnp.where(first, target_turned, target_near)
        printed = jax.nn.sigmoid(RESIST_SLOPE * (intensity - RESIST_LEVEL))
        at = low_lane + (start + side * STEP)
        valid = (at >= 0) & (at < cols) & (row >= 0) & (row < bands * rows)
        slope[:, cut] = jnp.where(
            valid, (2.0 * RESIST_SLOPE) * (printed - wanted) * printed * (1.0 - printed), 0.0
        )

    grad_spec[...] = jnp.zeros_like(grad_spec)

    def grad_unit(kernel):
        pair, member = kernel // 2, kernel % 2
        work = work_b.at[pair % BUFFERS]
        span = slice(member * SIZE, (member + 1) * SIZE)
        mixed = right_dot(slope[...] * field(kernel), cols_fwd)
        yield
        for half_at, part in enumerate(split(mixed)):
            for index in range(outs):
                at = slice(index * STEP, index * STEP + SIZE)
                work[index, half_at, 0:SIZE, span] = part[at, :SIZE]
                work[index, half_at, SIZE:, span] = part[at, SIZE:]
        if member == 0:
            return
        yield
        for index in range(outs):
            spec = left_dot(rows_fwd, (work[index, 0], work[index, 1]))
            yield
            cut = slice(index * SIZE, (index + 1) * SIZE)
            sum_re = grad_spec[0:SIZE, cut]
            sum_im = grad_spec[SIZE:, cut]
            for late_member in range(2):
                span = slice(late_member * SIZE, (late_member + 1) * SIZE)
                kern_re = spectra[2 * pair + late_member][0:SIZE]
                kern_im = spectra[2 * pair + late_member][SIZE:]
                spec_re = spec[0:SIZE, span]
                spec_im = spec[SIZE:, span]
                sum_re = sum_re + kern_re * spec_re + kern_im * spec_im
                sum_im = sum_im + kern_re * spec_im - kern_im * spec_re
            grad_spec[0:SIZE, cut] = sum_re
            grad_spec[SIZE:, cut] = sum_im

    staggered(grad_unit(kernel) for kernel in range(count))

    halfway = left_dot(grad_rows, split(grad_spec[...]))
    stacked = jnp.concatenate(
        [
            jnp.concatenate(
                [
                    halfway[0:STEP, index * SIZE:(index + 1) * SIZE],
                    halfway[STEP:, index * SIZE:(index + 1) * SIZE],
                ],
                axis=1,
            )
            for index in range(outs)
        ],
        axis=0,
    )
    high, low = split(stacked)
    both = dot(high, grad_cols[:, :SIZE])
    gradient = both[:, :STEP] + (both[:, STEP:] + dot(low, grad_cols[:, :STEP]))
    mask_share = pltpu.roll(
        jax.nn.sigmoid(MASK_SLOPE * logit_ref[...]), lax.rem(cols - place * STEP, cols), 1
    )[:, :STEP]
    out_ref[...] = jnp.transpose(
        gradient * (2.0 * MASK_SLOPE) * mask_share * (1.0 - mask_share)
    )


def body(mask_logit, target, kern_real, kern_imag, kern_weight):
    rows, cols = mask_logit.shape
    local, tap_count, _ = kern_real.shape
    reach = tap_count - 1
    kern_size = lax.axis_size("kern")
    tile_size = lax.axis_size("tile")
    assert reach == SIZE - STEP and cols == STEP * kern_size and rows % STEP == 0
    assert kern_size == 4 and rows == SIZE
    half = reach // 2
    vmem = pl.BlockSpec(memory_space=pltpu.VMEM)
    smem = pl.BlockSpec(memory_space=pltpu.SMEM)


    even, odd, taps = pl.pallas_call(
        pack_kernel,
        out_shape=(
            jax.ShapeDtypeStruct((2 * reach, SIZE), F32),
            jax.ShapeDtypeStruct((2 * reach, SIZE), F32),
            jax.ShapeDtypeStruct((local, TAP_ROWS, SIZE), F32),
        ),
        in_specs=[smem] + [vmem] * 4,
        out_specs=(vmem,) * 3,
    )(kern_weight, mask_logit, target, kern_real, kern_imag)

    def swaps(first):
        return [p for i in range(first, tile_size - 1, 2) for p in ((i, i + 1), (i + 1, i))]

    def flipped(value, flip):
        return lax.ppermute(value, "kern", [(i, i ^ flip) for i in range(kern_size)])

    far = flipped(taps, 2)
    near = flipped(taps, 1)
    even = lax.ppermute(even, "tile", swaps(0))
    odd = lax.ppermute(odd, "tile", swaps(1))
    both = flipped(far, 1)

    table = pl.pallas_call(
        table_kernel,
        out_shape=jax.ShapeDtypeStruct((sum(TABLE_ROWS), 2 * SIZE), BF16),
        out_specs=vmem,
        compiler_params=pltpu.CompilerParams(vmem_limit_bytes=8 * 1024 * 1024),
        cost_estimate=pl.CostEstimate(flops=2 * 10**9, bytes_accessed=5 * 10**6, transcendentals=0),
    )()
    field_rows = rows + reach
    windows = field_rows // STEP
    outs = rows // STEP
    count = local * kern_size
    early = count - local
    local_out = pl.pallas_call(
        local_kernel,
        out_shape=(
            jax.ShapeDtypeStruct((early, 2 * SIZE, SIZE), F32),
            jax.ShapeDtypeStruct((2, 2, rows, 2 * SIZE), BF16),
            jax.ShapeDtypeStruct((2 * SIZE, 2 * SIZE), F32),
            jax.ShapeDtypeStruct((early, STEP, 2 * SIZE), F32),
            jax.ShapeDtypeStruct((STEP, 2 * SIZE), F32),
        ),
        in_specs=[vmem] * 5,
        out_specs=(vmem,) * 5,
        scratch_shapes=[
            pltpu.VMEM((early * TAP_ROWS, 4 * SIZE), BF16),
            pltpu.VMEM((BUFFERS, 2, 2 * SIZE, 2 * SIZE), BF16),
            pltpu.VMEM((BUFFERS, 2, 2 * STEP, 2 * SIZE), BF16),
        ],
        compiler_params=pltpu.CompilerParams(vmem_limit_bytes=16 * 1024 * 1024),
        cost_estimate=pl.CostEstimate(flops=4 * 10**9, bytes_accessed=5 * 10**6, transcendentals=0),
    )(mask_logit, taps, near, far, table)
    result = pl.pallas_call(
        main_kernel,
        out_shape=jax.ShapeDtypeStruct((STEP, rows), F32),
        in_specs=[vmem] * (6 + len(local_out)),
        out_specs=vmem,
        scratch_shapes=[
            pltpu.VMEM((local, 2 * SIZE, SIZE), F32),
            pltpu.VMEM((windows, 2 * SIZE, 2 * SIZE), F32),
            pltpu.VMEM((count, field_rows, 2 * SIZE), F32),
            pltpu.VMEM((field_rows, 2 * SIZE), F32),
            pltpu.VMEM((field_rows, 2 * SIZE), F32),
            pltpu.VMEM((local * TAP_ROWS, 4 * SIZE), BF16),
            pltpu.VMEM((BUFFERS, 2, 2 * SIZE, 2 * SIZE), BF16),
            pltpu.VMEM((BUFFERS, 2, 2 * windows * STEP, 2 * SIZE), BF16),
            pltpu.VMEM((BUFFERS, outs, 2, 2 * SIZE, 2 * SIZE), BF16),
            pltpu.VMEM((2 * SIZE, outs * SIZE), F32),
        ],
        compiler_params=pltpu.CompilerParams(vmem_limit_bytes=24 * 1024 * 1024),
    )(mask_logit, target, even, odd, both, table, *local_out)
    return jnp.transpose(result)


def solution(mesh):
    in_specs = (
        P("tile", None),
        P("tile", None),
        P("kern", None, None),
        P("kern", None, None),
        P("kern"),
    )
    out_specs = P("tile", "kern")
    return jax.shard_map(body, mesh=mesh, in_specs=in_specs, out_specs=out_specs, check_vma=False)
```
